512 devices in a mesh: dp: 16 (over x, y), ctx: 32 (over z, core).
Axes of the slice: x: 4, y: 4, z: 16, core: 2. Of those that a mesh axis runs over, the one named last changes fastest.
Arguments:
- inputs: bfloat16 [16, 4096, 2560], P('dp', 'ctx'), may hold values from -6 to 6
- in_keys: bfloat16 [16, 4096, 128], P('dp', 'ctx'), may hold values from -6 to 6
- output_queries: bfloat16 [16, 4096, 128], P('dp', 'ctx'), may hold values from -0.5 to 0.5
- step_raw: float32 [16, 4096, 40], P('dp', 'ctx'), may hold values from -9 to 18
- decay_log: float32 [40], replicated, may hold values from -12 to 4
- skip_weight: float32 [40], replicated, may hold values from 0.5 to 1.5
- grad_out: bfloat16 [16, 4096, 2560], P('dp', 'ctx')
Outputs:
- grad_inputs: bfloat16 [16, 4096, 2560], P('dp', 'ctx')
- grad_keys: float32 [16, 4096, 128], P('dp', 'ctx')
- grad_queries: float32 [16, 4096, 128], P('dp', 'ctx')
- grad_steps: float32 [16, 4096, 40], P('dp', 'ctx')
- grad_decay: float32 [40], replicated
- grad_skip: float32 [40], replicated
The draws below stay inside these ranges and needn't reach their ends.
All inputs are finite; a program needn't handle non-finite values.
Results may differ from the reference program's by a relative error of at most 0.0035.
Values sent between devices are 32-bit elements; how exact they have to be, the bound alone decides.
No kernel may reach another device: no remote copies, remote signals or barrier semaphores. Data moves between devices by JAX's collectives and lax.ppermute only.
A program may use at most 128 MiB of HBM per device.

```python
import jax
import jax.numpy as jnp
from jax import lax

HEAD_SUBSET = 40
HEAD_DIM = 64
STATE = 128
TOK_DEV = 128
GENOME_LENGTH = 4096
GENOME_COUNT = 16
N_CTX = 32


base_step = 0.001


def head_rates(key):
    first_key, second_key, third_key, fourth_key = jax.random.split(jax.random.fold_in(key, 11), 4)
    chooser = jax.random.uniform(first_key, (HEAD_SUBSET,), jnp.float32)
    fast_share = 0.25
    medium_share = 0.5
    chain_loss = jnp.exp(jax.random.uniform(second_key, (HEAD_SUBSET,), jnp.float32, jnp.log(0.15), jnp.log(0.45)))
    fast_loss = jnp.exp(jax.random.uniform(third_key, (HEAD_SUBSET,), jnp.float32, jnp.log(1.0 / 50.0), jnp.log(1.0 / 30.0)))
    middling_objective = jnp.exp(jax.random.uniform(fourth_key, (HEAD_SUBSET,), jnp.float32, jnp.log(0.15), jnp.log(0.4)))
    slow_rate = chain_loss / (GENOME_LENGTH * base_step)
    medium_rate = middling_objective / (TOK_DEV * base_step)
    fast_rate = fast_loss / base_step
    return jnp.where(chooser < fast_share, fast_rate, jnp.where(chooser < medium_share, medium_rate, slow_rate))


def draw_decay_log(key, part):
    return jnp.log(head_rates(key)).astype(jnp.float32)


def draw_step_raw(key, part):
    spike_scale = head_rates(key)
    slab_count = GENOME_LENGTH // TOK_DEV
    rough_key, block_key, rank_key, offset_key, loss_random_key = jax.random.split(jax.random.fold_in(key, 23), 5)
    rough = jnp.exp(jax.random.uniform(rough_key, (GENOME_COUNT, GENOME_LENGTH, HEAD_SUBSET), jnp.float32, -0.7, 0.7))
    block_factor = jnp.exp(jax.random.uniform(block_key, (GENOME_COUNT, slab_count, 1, HEAD_SUBSET), jnp.float32, -0.7, 0.7))
    block_factor = jnp.broadcast_to(block_factor, (GENOME_COUNT, slab_count, TOK_DEV, HEAD_SUBSET)).reshape(GENOME_COUNT, GENOME_LENGTH, HEAD_SUBSET)
    typical_step = base_step * rough * block_factor
    rank_scores = jax.random.randint(rank_key, (GENOME_COUNT, slab_count, HEAD_SUBSET), 0, 2 ** 20) * slab_count
    rank_scores = rank_scores + jnp.arange(slab_count, dtype=jnp.int32)[None, :, None]
    ordering = jnp.argsort(rank_scores, axis=1)
    ascending_arrangement = jnp.argsort(ordering, axis=1)
    surge_intervals = ascending_arrangement < 3
    beginning_displacements = jax.random.randint(offset_key, (GENOME_COUNT, slab_count, HEAD_SUBSET), 0, TOK_DEV)
    dot_contraction = jnp.arange(TOK_DEV, dtype=jnp.int32)
    peak_coordinates = surge_intervals[:, :, None, :] & (dot_contraction[None, None, :, None] == beginning_displacements[:, :, None, :])
    peak_coordinates = peak_coordinates.reshape(GENOME_COUNT, GENOME_LENGTH, HEAD_SUBSET)
    spike_loss = jax.random.uniform(loss_random_key, (GENOME_COUNT, GENOME_LENGTH, HEAD_SUBSET), jnp.float32, 0.22, 0.6)
    spike_step = spike_loss / spike_scale[None, None, :]
    step_widths = jnp.where(peak_coordinates, spike_step, typical_step)
    return jnp.log(jnp.expm1(step_widths)).astype(jnp.float32)


def draw_grad_out(key, part):
    noise_key = jax.random.fold_in(key, 5)
    shape = (GENOME_COUNT, GENOME_LENGTH, HEAD_SUBSET * HEAD_DIM)
    along = jnp.arange(GENOME_LENGTH, dtype=jnp.float32) / max(GENOME_LENGTH - 1, 1)
    across = jnp.arange(GENOME_COUNT, dtype=jnp.float32) / max(GENOME_COUNT - 1, 1)
    scale = (1.0 + 2.0 * across)[:, None, None] * (1.0 + 2.0 * along)[None, :, None]
    values = jax.random.normal(noise_key, shape, jnp.float32)
    return (values * scale).astype(jnp.bfloat16)


def levels(stream_key, shape, cuts, least, largest):
    def one(axis_at, parts):
        steps = jax.random.uniform(jax.random.fold_in(jax.random.fold_in(stream_key, 6), axis_at), (parts,), jnp.float32, least / len(cuts), largest / len(cuts))
        return jnp.repeat(jnp.exp(steps), shape[axis_at] // parts).reshape((-1,) + (1,) * (len(shape) - axis_at - 1))

    loudness = one(*cuts[0])
    for cut in cuts[1:]:
        loudness = loudness * one(*cut)
    return loudness


def scatter_about(rng, dims, deviation, limit, cuts=(), kind=jnp.bfloat16):
    array = deviation * jax.random.normal(rng, dims, jnp.float32)
    if cuts:
        array = array * levels(rng, dims, cuts, -0.22, 0.18)
    return jnp.clip(array, -limit, limit).astype(kind)


def setup_inputs(seed: int = 0) -> dict:
    arg_keys = jax.random.split(jax.random.key(seed), 8)
    return {
        "inputs": scatter_about(arg_keys[0], (GENOME_COUNT, GENOME_LENGTH, HEAD_SUBSET * HEAD_DIM), 1.0, 6.0, ((0, 16), (1, 32))),
        "in_keys": scatter_about(arg_keys[1], (GENOME_COUNT, GENOME_LENGTH, STATE), 1.0, 6.0, ((0, 16), (1, 32))),
        "output_queries": scatter_about(arg_keys[2], (GENOME_COUNT, GENOME_LENGTH, STATE), STATE ** -0.5, 0.5, ((0, 16), (1, 32))),
        "step_raw": draw_step_raw(jax.random.fold_in(arg_keys[7], 71), 0),
        "decay_log": draw_decay_log(jax.random.fold_in(arg_keys[7], 71), 0),
        "skip_weight": jnp.clip(jax.random.uniform(arg_keys[5], (HEAD_SUBSET,), jnp.float32, 0.5, 1.5), 0.5, 1.5),
        "grad_out": draw_grad_out(jax.random.fold_in(arg_keys[7], 71), 0),
    }


def forward_genome(inputs_f, keys_f, queries_f, raw_steps, decay_log, skip_weight):
    step_widths = jax.nn.softplus(raw_steps)
    decay_rates = -jnp.exp(decay_log)
    log_decay = step_widths * decay_rates[None, :]
    token_place = jnp.arange(TOK_DEV)
    causal = token_place[:, None] >= token_place[None, :]
    inputs_c = inputs_f.reshape(N_CTX, TOK_DEV, HEAD_SUBSET, HEAD_DIM)
    keys_c = keys_f.reshape(N_CTX, TOK_DEV, STATE)
    queries_c = queries_f.reshape(N_CTX, TOK_DEV, STATE)
    steps_c = step_widths.reshape(N_CTX, TOK_DEV, HEAD_SUBSET)
    decay_c = log_decay.reshape(N_CTX, TOK_DEV, HEAD_SUBSET)

    def advance(carry_state, slab):
        inputs_s, keys_s, queries_s, steps_s, decay_s = slab
        cumulative = jnp.cumsum(decay_s, axis=0)
        between = cumulative[:, None, :] - cumulative[None, :, :]
        segment_decay = jnp.exp(jnp.where(causal[:, :, None], between, -jnp.inf))
        scores = jnp.dot(queries_s, keys_s.T, precision=lax.Precision.HIGHEST)
        kernel = segment_decay * scores[:, :, None] * steps_s[None, :, :]
        outputs = jnp.einsum('ijh,jhp->ihp', kernel, inputs_s, precision=lax.Precision.HIGHEST)
        outputs = outputs + jnp.exp(cumulative)[:, :, None] * jnp.einsum('in,hpn->ihp', queries_s, carry_state, precision=lax.Precision.HIGHEST)
        outputs = outputs + skip_weight[None, :, None] * inputs_s
        closing_segment = cumulative[-1]
        weighted = (jnp.exp(closing_segment[None, :] - cumulative) * steps_s)[:, :, None] * inputs_s
        new_state = jnp.exp(closing_segment)[:, None, None] * carry_state + jnp.einsum('jhp,jn->hpn', weighted, keys_s, precision=lax.Precision.HIGHEST)
        return (new_state, outputs)
    start_state = jnp.zeros((HEAD_SUBSET, HEAD_DIM, STATE), jnp.float32)
    final_state, outputs = lax.scan(advance, start_state, (inputs_c, keys_c, queries_c, steps_c, decay_c))
    return outputs.reshape(GENOME_LENGTH, HEAD_SUBSET, HEAD_DIM)

def reference(inputs, in_keys, output_queries, step_raw, decay_log, skip_weight, grad_out):

    def one_genome(slab):
        inputs_g, keys_g, queries_g, raw_g, cotangent_g = slab
        inputs_f = inputs_g.astype(jnp.float32).reshape(GENOME_LENGTH, HEAD_SUBSET, HEAD_DIM)
        keys_f = keys_g.astype(jnp.float32)
        queries_f = queries_g.astype(jnp.float32)
        cotangent = cotangent_g.astype(jnp.float32).reshape(GENOME_LENGTH, HEAD_SUBSET, HEAD_DIM)
        result, pullback = jax.vjp(forward_genome, inputs_f, keys_f, queries_f, raw_g, decay_log, skip_weight)
        grads = pullback(cotangent)
        grad_in = grads[0].reshape(GENOME_LENGTH, HEAD_SUBSET * HEAD_DIM).astype(jnp.bfloat16)
        return (grad_in, grads[1], grads[2], grads[3], grads[4], grads[5])
    outcome = lax.map(one_genome, (inputs, in_keys, output_queries, step_raw, grad_out))
    return (outcome[0], outcome[1], outcome[2], outcome[3], lax.optimization_barrier(jnp.sum(outcome[4], axis=0)), lax.optimization_barrier(jnp.sum(outcome[5], axis=0)))
```

```python
import functools

import jax
import jax.numpy as jnp
from jax import lax
from jax.experimental import pallas as pl
from jax.experimental.pallas import tpu as pltpu
from jax.sharding import PartitionSpec as P

F32 = jnp.float32
BF16 = jnp.bfloat16
HIGHEST = lax.Precision.HIGHEST
LANES = 128
STREAMS = 2
VMEM_LIMIT = 48 * 1024 * 1024


def nn(a, b):
    return lax.dot_general(a, b, (((1,), (0,)), ((), ())), preferred_element_type=F32)


def nt(a, b):
    return lax.dot_general(a, b, (((1,), (1,)), ((), ())), preferred_element_type=F32)


def halves(a):
    high = a.astype(BF16)
    low = (a - high.astype(F32)).astype(BF16)
    return high, low


def iota(shape, dim):
    return lax.broadcasted_iota(jnp.int32, shape, dim)


def spread(values, block, first):
    return jnp.where(first, values[:, 2 * block : 2 * block + 1], values[:, 2 * block + 1 : 2 * block + 2])


def head_terms(raw_ref, decay_ref, wide, heads):
    rows = raw_ref.shape[0]
    wide[...] = jnp.zeros_like(wide)
    wide[0:1, :heads] = decay_ref[...]
    rate = jnp.where(iota((1, LANES), 1) < heads, -jnp.exp(wide[0:1, :]), 0.0)
    wide[0:1, :] = jnp.zeros((1, LANES), F32)
    wide[:, :heads] = raw_ref[...]
    raw = wide[...]
    step = jnp.maximum(raw, 0.0) + jnp.log1p(jnp.exp(-jnp.abs(raw)))
    lower = (iota((rows, rows), 0) >= iota((rows, rows), 1)).astype(F32)
    cumulative = jnp.dot(lower, step * rate, precision=HIGHEST, preferred_element_type=F32)
    return raw, step, rate, cumulative


def summary_kernel(heads, blocks, core_ref, raw_ref, decay_ref, x_ref, g_ref, b_ref, c_ref, *rest):
    keeps, sends, wide = rest[:STREAMS], rest[STREAMS : 2 * STREAMS], rest[2 * STREAMS]
    forward = core_ref[0] == 1
    raw, step, rate, cumulative = head_terms(raw_ref, decay_ref, wide, heads)
    closing = cumulative[-1:, :]
    weight = jnp.exp(closing - cumulative) * step
    lift = jnp.exp(cumulative)
    rows = cumulative.shape[0]
    first = iota((rows, LANES), 1) < LANES // 2
    keys_t = b_ref[...].astype(F32).T.astype(BF16)
    queries_t = c_ref[...].astype(F32).T.astype(BF16)
    keys_t = jnp.concatenate([keys_t, keys_t], axis=1)
    queries_t = jnp.concatenate([queries_t, queries_t], axis=1)
    per = blocks // STREAMS
    for block in range(blocks):
        stream, place = block // per, block % per
        cols = pl.ds(block * LANES, LANES)
        weighted = spread(weight, block, first) * x_ref[:, cols].astype(F32)
        lifted = spread(lift, block, first) * g_ref[:, cols].astype(F32)
        state = nn(keys_t, jnp.concatenate(halves(weighted), axis=0))
        message = nn(queries_t, jnp.concatenate(halves(lifted), axis=0))
        where = pl.ds(place * LANES, LANES)
        keeps[stream][where, :] = jnp.where(forward, state, message)
        sends[stream][where, :] = jnp.where(forward, message, state)
    for stream in range(STREAMS):
        extra = keeps[stream].shape[0] - per * LANES
        logs = [
            spread(closing, stream * per + place, first[:1]) for place in range(per)
        ] + [jnp.zeros((extra - per, LANES), F32)]
        logs = jnp.concatenate(logs, axis=0)
        keeps[stream][pl.ds(per * LANES, extra), :] = logs
        sends[stream][pl.ds(per * LANES, extra), :] = logs


def local_kernel(
    heads,
    blocks,
    raw_ref,
    decay_ref,
    x_ref,
    g_ref,
    b_ref,
    c_ref,
    adjoint_ref,
    keys_ref,
    queries_ref,
    through_ref,
    column_ref,
    step_ref,
    cumulative_ref,
    slope_ref,
    rate_ref,
    skip_ref,
    wide,
    row_t,
):
    raw, step, rate, cumulative = head_terms(raw_ref, decay_ref, wide, heads)
    rows = cumulative.shape[0]
    lane = iota((rows, LANES), 1)
    first = lane < LANES // 2
    causal = iota((rows, rows), 1) >= iota((rows, rows), 0)
    cumulative_t = cumulative.T
    keys = b_ref[...]
    queries = c_ref[...]
    scores_t = jnp.where(causal, nt(keys, queries), 0.0)
    row_t[...] = jnp.zeros_like(row_t)
    gathered = jnp.zeros((rows, rows), F32)
    column_step = jnp.zeros((rows, LANES), F32)
    skip = jnp.zeros((1, LANES), F32)
    lane_one = iota((1, LANES), 1)
    zero = jnp.zeros((rows, LANES), BF16)
    for block in range(blocks):
        cols = pl.ds(block * LANES, LANES)
        x = x_ref[:, cols]
        g = g_ref[:, cols]
        both_x = jnp.concatenate([jnp.where(first, x, zero), jnp.where(first, zero, x)], axis=0)
        both_g = jnp.concatenate([jnp.where(first, g, zero), jnp.where(first, zero, g)], axis=0)
        products = nt(both_x, g)
        highs, lows = [], []
        for half in range(2):
            head = 2 * block + half
            between = cumulative_t[head : head + 1, :] - cumulative[:, head : head + 1]
            decay = jnp.exp(jnp.minimum(between, 0.0))
            high, low = halves(decay * scores_t)
            highs.append(high)
            lows.append(low)
            scaled = decay * products[half * rows : (half + 1) * rows] * step[:, head : head + 1]
            gathered = gathered + scaled
            scored = scaled * scores_t
            row_t[head : head + 1, :] = jnp.sum(scored, axis=0, keepdims=True)
            column_step = jnp.where(lane == head, jnp.sum(scored, axis=1, keepdims=True), column_step)
        adjoint_ref[:, cols] = nn(jnp.concatenate(highs, axis=1), both_g) + nn(
            jnp.concatenate(lows, axis=1), both_g
        )
        met = jnp.sum(x.astype(F32) * g.astype(F32), axis=0, keepdims=True)
        early = jnp.sum(jnp.where(first[:1], met, 0.0), axis=1, keepdims=True)
        late = jnp.sum(jnp.where(first[:1], 0.0, met), axis=1, keepdims=True)
        skip = jnp.where(lane_one == 2 * block, early, skip)
        skip = jnp.where(lane_one == 2 * block + 1, late, skip)
    gathered = jnp.where(causal, gathered, 0.0)
    keys_ref[...] = nn(
        jnp.concatenate(halves(gathered), axis=1), jnp.concatenate([queries, queries], axis=0)
    )
    queries_ref[...] = nn(
        jnp.concatenate(halves(gathered.T), axis=1), jnp.concatenate([keys, keys], axis=0)
    )
    through_ref[...] = row_t[...].T - column_step
    column_ref[...] = column_step / step
    step_ref[...] = step
    cumulative_ref[...] = cumulative
    slope_ref[...] = 1.0 / (1.0 + jnp.exp(-raw))
    rate_ref[...] = rate
    skip_ref[...] = skip


def finish_kernel(
    heads,
    blocks,
    core_ref,
    skip_weight_ref,
    x_ref,
    g_ref,
    b_ref,
    c_ref,
    adjoint_ref,
    keys_in,
    queries_in,
    through_ref,
    column_ref,
    step_ref,
    cumulative_ref,
    slope_ref,
    rate_ref,
    skip_ref,
    *rest,
):
    pairs, before, other = (rest[i * STREAMS : (i + 1) * STREAMS] for i in range(3))
    grad_x, grad_keys, grad_queries, grad_raw, sums, wide = rest[3 * STREAMS :]
    forward = core_ref[0] == 1
    step = step_ref[...]
    cumulative = cumulative_ref[...]
    rate = rate_ref[...]
    rows = cumulative.shape[0]
    wide[...] = jnp.zeros_like(wide)
    wide[0:1, :heads] = skip_weight_ref[...]
    skip_weight = wide[0:1, :]
    closing = cumulative[-1:, :]
    tail = jnp.exp(closing - cumulative)
    lift = jnp.exp(cumulative)
    first = iota((rows, LANES), 1) < LANES // 2
    lane_one = iota((1, LANES), 1)
    keys = jnp.concatenate([b_ref[...], b_ref[...]], axis=1)
    queries = jnp.concatenate([c_ref[...], c_ref[...]], axis=1)
    side = iota((LANES, LANES), 0) // (LANES // 2)
    place_lane = iota((LANES, LANES), 1)
    per = blocks // STREAMS
    from_keys = keys_in[...]
    from_queries = queries_in[...]
    outward_sum = jnp.zeros((rows, LANES), F32)
    inward_sum = jnp.zeros((rows, LANES), F32)
    meeting = jnp.zeros((1, LANES), F32)
    for block in range(blocks):
        stream, place = block // per, block % per
        cols = pl.ds(block * LANES, LANES)
        where = pl.ds(place * LANES, LANES)
        log_row = pairs[stream][pl.ds(per * LANES + place, 1), :]
        mine = pairs[stream][where, :] + jnp.exp(log_row) * before[stream][where, :]
        theirs = other[stream][where, :]
        entering = jnp.where(forward, mine, theirs)
        message = jnp.where(forward, theirs, mine)
        entering_high, entering_low = halves(entering)
        message_high, message_low = halves(message)
        x = x_ref[:, cols].astype(F32)
        g = g_ref[:, cols].astype(F32)
        message_keys = nn(keys, jnp.concatenate([message_high, message_low], axis=0))
        state_queries = nn(queries, jnp.concatenate([entering_high, entering_low], axis=0))
        tail_b = spread(tail, block, first)
        step_b = spread(step, block, first)
        skip_b = spread(skip_weight, block, first[:1])
        weighted_high, weighted_low = halves(tail_b * step_b * x)
        lifted_high, lifted_low = halves(spread(lift, block, first) * g)
        picker = jnp.where(place_lane == side + 2 * block, 1.0, 0.0).astype(BF16)
        picker = jnp.concatenate([picker, picker], axis=0)
        outward_sum = outward_sum + nn(jnp.concatenate(halves(x * message_keys), axis=1), picker)
        inward_sum = inward_sum + nn(jnp.concatenate(halves(g * state_queries), axis=1), picker)
        from_keys = from_keys + (
            nt(
                jnp.concatenate([weighted_high, weighted_low], axis=1),
                jnp.concatenate([message_high, message_high], axis=1),
            )
            + nt(weighted_high, message_low)
        )
        from_queries = from_queries + (
            nt(
                jnp.concatenate([lifted_high, lifted_low], axis=1),
                jnp.concatenate([entering_high, entering_high], axis=1),
            )
            + nt(lifted_high, entering_low)
        )
        met = jnp.sum(entering * message, axis=0, keepdims=True)
        early = jnp.sum(jnp.where(first[:1], met, 0.0), axis=1, keepdims=True)
        late = jnp.sum(jnp.where(first[:1], 0.0, met), axis=1, keepdims=True)
        meeting = jnp.where(lane_one == 2 * block, early, meeting)
        meeting = jnp.where(lane_one == 2 * block + 1, late, meeting)
        grad = step_b * (adjoint_ref[:, cols] + tail_b * message_keys) + skip_b * g
        grad_x[:, cols] = grad.astype(grad_x.dtype)
    grad_keys[...] = from_keys
    grad_queries[...] = from_queries
    inward = lift * inward_sum
    lead = tail * outward_sum
    outward = lead * step
    through = through_ref[...] + inward - outward
    last = jnp.sum(outward, axis=0, keepdims=True) + jnp.exp(closing) * meeting
    through = through + jnp.where(iota((rows, LANES), 0) == rows - 1, last, 0.0)
    upper = (iota((rows, rows), 1) >= iota((rows, rows), 0)).astype(F32)
    grad_cumulative = jnp.dot(upper, through, precision=HIGHEST, preferred_element_type=F32)
    grad_step = grad_cumulative * rate + column_ref[...] + lead
    grad_raw[...] = (grad_step * slope_ref[...])[:, :heads]
    rate_sum = jnp.sum(grad_cumulative * step, axis=0, keepdims=True) * rate
    sums[0:1, :] = jnp.where(lane_one < heads, rate_sum, 0.0)
    sums[1:2, :] = jnp.where(lane_one < heads, skip_ref[...], 0.0)


def chip_moves(moves, chips):
    ahead = [(2 * a + 1, 2 * b + 1) for a, b in moves]
    back = [(2 * (chips - 1 - a), 2 * (chips - 1 - b)) for a, b in moves]
    return ahead + back


ROUNDS = (
    [(z, z + 1) for z in range(0, 16, 2)],
    [(1, 3), (5, 7), (9, 11), (13, 15)],
    [(3, 7), (1, 2)],
    [(7, 11), (3, 5)],
    [(11, 13), (7, 9), (5, 6), (3, 4)],
    [(7, 8), (9, 10), (11, 12), (13, 14)],
)
LAST_CHIP = [(11, 15)]


def open_up(buffer, per):
    state = buffer[: per * LANES].reshape(per, LANES, LANES)
    log = buffer[per * LANES : per * LANES + per].reshape(per, 1, LANES)
    return state, log


def close_up(state, log, rows):
    per = state.shape[0]
    pad = jnp.zeros((rows - per * LANES - per, LANES), F32)
    return jnp.concatenate([state.reshape(per * LANES, LANES), log.reshape(per, LANES), pad], axis=0)


def scan_chips(keeps, pairs, per, swap):
    chips = 16
    rows = keeps[0].shape[0]
    own, before = [], [None] * STREAMS
    for keep, pair in zip(keeps, pairs):
        state, log = open_up(keep, per)
        pair_state, pair_log = open_up(pair, per)
        own.append((state + jnp.exp(log) * pair_state, log + pair_log))
    for turn, moves in enumerate(ROUNDS):
        arrived = []
        for stream in range(STREAMS):
            state, log = own[stream]
            if before[stream] is not None:
                past, past_log = before[stream]
                state, log = state + jnp.exp(log) * past, log + past_log
            if turn < 3:
                packed = close_up(state, log, rows)
                arrived.append([open_up(lax.ppermute(packed, "ctx", chip_moves(moves, chips)), per)])
            else:
                got = [(lax.ppermute(state, "ctx", chip_moves(moves, chips)), None)]
                if turn == 4:
                    got.append((lax.ppermute(state, "ctx", chip_moves(LAST_CHIP, chips)), None))
                arrived.append(got)
        for stream in range(STREAMS):
            for state, log in arrived[stream]:
                if before[stream] is None:
                    before[stream] = (state, log)
                else:
                    past, past_log = before[stream]
                    new_log = past_log if log is None else past_log + log
                    before[stream] = (past + jnp.exp(past_log) * state, new_log)
    flat = [past.reshape(per * LANES, LANES) for past, _ in before]
    return flat, [lax.ppermute(past, "ctx", swap) for past in flat]


def per_device(inputs, in_keys, output_queries, step_raw, decay_log, skip_weight, grad_out):
    rows = inputs.shape[1]
    width = inputs.shape[2]
    heads = decay_log.shape[0]
    blocks = width // LANES
    per = blocks // STREAMS
    extra = (per + 7) // 8 * 8
    count = lax.axis_size("ctx")
    swap = [(i, i ^ 1) for i in range(count)]
    core = lax.rem(lax.axis_index("ctx"), 2).astype(jnp.int32).reshape(1)
    x, g, keys, queries, raw = inputs[0], grad_out[0], in_keys[0], output_queries[0], step_raw[0]
    decay_row = decay_log.reshape(1, heads)
    skip_row = skip_weight.reshape(1, heads)
    whole = pl.BlockSpec(memory_space=pltpu.VMEM)
    scalar = pl.BlockSpec(memory_space=pltpu.SMEM)
    params = pltpu.CompilerParams(vmem_limit_bytes=VMEM_LIMIT)
    tile = jax.ShapeDtypeStruct((rows, LANES), F32)
    line = jax.ShapeDtypeStruct((1, LANES), F32)
    packed = jax.ShapeDtypeStruct((per * LANES + extra, LANES), F32)
    wide = pltpu.VMEM((rows, LANES), F32)

    made = pl.pallas_call(
        functools.partial(summary_kernel, heads, blocks),
        out_shape=[packed] * (2 * STREAMS),
        in_specs=[scalar] + [whole] * 6,
        out_specs=[whole] * (2 * STREAMS),
        scratch_shapes=[wide],
        compiler_params=params,
        cost_estimate=pl.CostEstimate(flops=400_000_000, bytes_accessed=4_000_000, transcendentals=0),
        name="summaries",
    )(core, raw, decay_row, x, g, keys, queries)
    keeps, sends = made[:STREAMS], made[STREAMS:]
    local = pl.pallas_call(
        functools.partial(local_kernel, heads, blocks),
        out_shape=[jax.ShapeDtypeStruct((rows, width), F32)] + [tile] * 7 + [line] * 2,
        in_specs=[whole] * 6,
        out_specs=[whole] * 10,
        scratch_shapes=[wide, pltpu.VMEM((LANES, rows), F32)],
        compiler_params=params,
        cost_estimate=pl.CostEstimate(flops=2_000_000_000, bytes_accessed=4_000_000, transcendentals=0),
        name="within_slab",
    )(raw, decay_row, x, g, keys, queries)
    pairs = [lax.ppermute(send, "ctx", swap) for send in sends]
    before, other = scan_chips(keeps, pairs, per, swap)
    grad_x, grad_keys, grad_queries, grad_raw, sums = pl.pallas_call(
        functools.partial(finish_kernel, heads, blocks),
        out_shape=[
            jax.ShapeDtypeStruct((rows, width), BF16),
            tile,
            tile,
            jax.ShapeDtypeStruct((rows, heads), F32),
            jax.ShapeDtypeStruct((2, LANES), F32),
        ],
        in_specs=[scalar] + [whole] * (15 + 3 * STREAMS),
        out_specs=[whole] * 5,
        scratch_shapes=[wide],
        compiler_params=params,
        cost_estimate=pl.CostEstimate(flops=800_000_000, bytes_accessed=8_000_000, transcendentals=0),
        name="gradients",
    )(core, skip_row, x, g, keys, queries, *local, *pairs, *before, *other)
    line_sum = jnp.concatenate([sums[0, : LANES // 2], sums[1, : LANES // 2]])
    for axis in ("ctx", "dp"):
        size = lax.axis_size(axis)
        shared = jnp.broadcast_to(line_sum[None], (size, LANES))
        line_sum = jnp.sum(lax.all_to_all(shared, axis, 0, 0, tiled=True), axis=0)
    return (
        grad_x[None],
        grad_keys[None],
        grad_queries[None],
        grad_raw[None],
        line_sum[:heads],
        line_sum[LANES // 2 : LANES // 2 + heads],
    )


def solution(mesh):
    placed = P("dp", "ctx", None)
    return jax.shard_map(
        per_device,
        mesh=mesh,
        in_specs=(placed, placed, placed, placed, P(), P(), placed),
        out_specs=(placed, placed, placed, placed, P(), P()),
        check_vma=False,
    )
```

```python
import functools

import jax
import jax.numpy as jnp
from jax import lax
from jax.experimental import pallas as pl
from jax.experimental.pallas import tpu as pltpu
from jax.sharding import PartitionSpec as P

F32 = jnp.float32
BF16 = jnp.bfloat16
HIGHEST = lax.Precision.HIGHEST
LANES = 128
STREAMS = 2
VMEM_LIMIT = 20 * 1024 * 1024


def nn(a, b):
    return lax.dot_general(a, b, (((1,), (0,)), ((), ())), preferred_element_type=F32)


def nt(a, b):
    return lax.dot_general(a, b, (((1,), (1,)), ((), ())), preferred_element_type=F32)


def halves(a):
    high = a.astype(BF16)
    low = (a - high.astype(F32)).astype(BF16)
    return high, low


def iota(shape, dim):
    return lax.broadcasted_iota(jnp.int32, shape, dim)


def spread(values, block, first):
    return jnp.where(first, values[:, 2 * block : 2 * block + 1], values[:, 2 * block + 1 : 2 * block + 2])


def head_terms(raw_ref, decay_ref, wide, heads):
    rows = raw_ref.shape[1]
    wide[...] = jnp.zeros_like(wide)
    wide[0:1, :heads] = decay_ref[...]
    rate = jnp.where(iota((1, LANES), 1) < heads, -jnp.exp(wide[0:1, :]), 0.0)
    wide[0:1, :] = jnp.zeros((1, LANES), F32)
    wide[:heads, :] = raw_ref[...]
    raw = wide[...].T
    step = jnp.maximum(raw, 0.0) + jnp.log1p(jnp.exp(-jnp.abs(raw)))
    lower = (iota((rows, rows), 0) >= iota((rows, rows), 1)).astype(F32)
    cumulative = jnp.dot(lower, step * rate, precision=HIGHEST, preferred_element_type=F32)
    return raw, step, rate, cumulative


def summary_kernel(heads, blocks, core_ref, raw_ref, decay_ref, x_ref, g_ref, b_ref, c_ref, *rest):
    keeps, sends, wide = rest[:STREAMS], rest[STREAMS : 2 * STREAMS], rest[2 * STREAMS]
    forward = core_ref[0] == 1
    raw, step, rate, cumulative = head_terms(raw_ref, decay_ref, wide, heads)
    closing = cumulative[-1:, :]
    weight = jnp.exp(closing - cumulative) * step
    lift = jnp.exp(cumulative)
    rows = cumulative.shape[0]
    first = iota((rows, LANES), 1) < LANES // 2
    keys_t = b_ref[...].astype(F32).T.astype(BF16)
    queries_t = c_ref[...].astype(F32).T.astype(BF16)
    keys_t = jnp.concatenate([keys_t, keys_t], axis=1)
    queries_t = jnp.concatenate([queries_t, queries_t], axis=1)
    per = blocks // STREAMS
    for block in range(blocks):
        stream, place = block // per, block % per
        cols = pl.ds(block * LANES, LANES)
        weighted = spread(weight, block, first) * x_ref[:, cols].astype(F32)
        lifted = spread(lift, block, first) * g_ref[:, cols].astype(F32)
        state = nn(keys_t, jnp.concatenate(halves(weighted), axis=0))
        message = nn(queries_t, jnp.concatenate(halves(lifted), axis=0))
        where = pl.ds(place * LANES, LANES)
        keeps[stream][where, :] = jnp.where(forward, state, message)
        sends[stream][where, :] = jnp.where(forward, message, state)
    for stream in range(STREAMS):
        extra = keeps[stream].shape[0] - per * LANES
        logs = [
            spread(closing, stream * per + place, first[:1]) for place in range(per)
        ] + [jnp.zeros((extra - per, LANES), F32)]
        logs = jnp.concatenate(logs, axis=0)
        keeps[stream][pl.ds(per * LANES, extra), :] = logs
        sends[stream][pl.ds(per * LANES, extra), :] = logs


def local_kernel(
    heads,
    blocks,
    raw_ref,
    decay_ref,
    x_ref,
    g_ref,
    b_ref,
    c_ref,
    adjoint_ref,
    keys_ref,
    queries_ref,
    through_ref,
    column_ref,
    step_ref,
    cumulative_ref,
    slope_ref,
    rate_ref,
    skip_ref,
    wide,
    row_t,
):
    raw, step, rate, cumulative = head_terms(raw_ref, decay_ref, wide, heads)
    rows = cumulative.shape[0]
    lane = iota((rows, LANES), 1)
    first = lane < LANES // 2
    causal = iota((rows, rows), 1) >= iota((rows, rows), 0)
    cumulative_t = cumulative.T
    keys = b_ref[...]
    queries = c_ref[...]
    scores_t = jnp.where(causal, nt(keys, queries), 0.0)
    row_t[...] = jnp.zeros_like(row_t)
    gathered = jnp.zeros((rows, rows), F32)
    column_step = jnp.zeros((rows, LANES), F32)
    skip = jnp.zeros((1, LANES), F32)
    lane_one = iota((1, LANES), 1)
    zero = jnp.zeros((rows, LANES), BF16)
    for block in range(blocks):
        cols = pl.ds(block * LANES, LANES)
        x = x_ref[:, cols]
        g = g_ref[:, cols]
        both_x = jnp.concatenate([jnp.where(first, x, zero), jnp.where(first, zero, x)], axis=0)
        both_g = jnp.concatenate([jnp.where(first, g, zero), jnp.where(first, zero, g)], axis=0)
        products = nt(both_x, g)
        highs, lows = [], []
        for half in range(2):
            head = 2 * block + half
            between = cumulative_t[head : head + 1, :] - cumulative[:, head : head + 1]
            decay = jnp.exp(jnp.minimum(between, 0.0))
            high, low = halves(decay * scores_t)
            highs.append(high)
            lows.append(low)
            scaled = decay * products[half * rows : (half + 1) * rows] * step[:, head : head + 1]
            gathered = gathered + scaled
            scored = scaled * scores_t
            row_t[head : head + 1, :] = jnp.sum(scored, axis=0, keepdims=True)
            column_step = jnp.where(lane == head, jnp.sum(scored, axis=1, keepdims=True), column_step)
        adjoint_ref[:, cols] = nn(jnp.concatenate(highs, axis=1), both_g) + nn(
            jnp.concatenate(lows, axis=1), both_g
        )
        met = jnp.sum(x.astype(F32) * g.astype(F32), axis=0, keepdims=True)
        early = jnp.sum(jnp.where(first[:1], met, 0.0), axis=1, keepdims=True)
        late = jnp.sum(jnp.where(first[:1], 0.0, met), axis=1, keepdims=True)
        skip = jnp.where(lane_one == 2 * block, early, skip)
        skip = jnp.where(lane_one == 2 * block + 1, late, skip)
    gathered = jnp.where(causal, gathered, 0.0)
    keys_ref[...] = nn(
        jnp.concatenate(halves(gathered), axis=1), jnp.concatenate([queries, queries], axis=0)
    )
    queries_ref[...] = nn(
        jnp.concatenate(halves(gathered.T), axis=1), jnp.concatenate([keys, keys], axis=0)
    )
    through_ref[...] = row_t[...].T - column_step
    column_ref[...] = column_step / step
    step_ref[...] = step
    cumulative_ref[...] = cumulative
    slope_ref[...] = 1.0 / (1.0 + jnp.exp(-raw))
    rate_ref[...] = rate
    skip_ref[...] = skip


def gradient_kernel(heads, blocks, stream, core_ref, skip_weight_ref, x_ref, g_ref, b_ref, c_ref, *rest):
    fixed, rest = rest[:9], rest[9:]
    (adjoint_ref, through_ref, column_ref, step_ref, cumulative_ref, slope_ref, rate_ref, skip_ref, pair_ref) = fixed
    before_ref, other_ref, rest = rest[0], rest[1], rest[2:]
    given = 2 if stream == 0 else 6
    taken, rest = rest[:given], rest[given:]
    final = stream == STREAMS - 1
    forward = core_ref[0] == 1
    step = step_ref[...]
    cumulative = cumulative_ref[...]
    rows = cumulative.shape[0]
    wide = rest[-1]
    wide[0:1, :] = jnp.zeros((1, LANES), F32)
    wide[0:1, :heads] = skip_weight_ref[...]
    skip_weight = wide[0:1, :]
    closing = cumulative[-1:, :]
    tail = jnp.exp(closing - cumulative)
    lift = jnp.exp(cumulative)
    first = iota((rows, LANES), 1) < LANES // 2
    lane_one = iota((1, LANES), 1)
    keys = jnp.concatenate([b_ref[...], b_ref[...]], axis=1)
    queries = jnp.concatenate([c_ref[...], c_ref[...]], axis=1)
    side = iota((LANES, LANES), 0) // (LANES // 2)
    place_lane = iota((LANES, LANES), 1)
    per = blocks // STREAMS
    from_keys = taken[0][...]
    from_queries = taken[1][...]
    if stream == 0:
        outward_sum = jnp.zeros((rows, LANES), F32)
        inward_sum = jnp.zeros((rows, LANES), F32)
        meeting = jnp.zeros((1, LANES), F32)
    else:
        outward_sum = taken[2][...]
        inward_sum = taken[3][...]
        meeting = taken[4][...]
    grad_x = rest[0]
    if stream > 0:
        ready = pl.ds(0, stream * per * LANES)
        grad_x[:, ready] = taken[5][:, ready]
    for place in range(per):
        block = stream * per + place
        cols = pl.ds(block * LANES, LANES)
        where = pl.ds(place * LANES, LANES)
        log_row = pair_ref[pl.ds(per * LANES + place, 1), :]
        mine = pair_ref[where, :] + jnp.exp(log_row) * before_ref[where, :]
        theirs = other_ref[where, :]
        entering = jnp.where(forward, mine, theirs)
        message = jnp.where(forward, theirs, mine)
        entering_high, entering_low = halves(entering)
        message_high, message_low = halves(message)
        x = x_ref[:, cols].astype(F32)
        g = g_ref[:, cols].astype(F32)
        message_keys = nn(keys, jnp.concatenate([message_high, message_low], axis=0))
        state_queries = nn(queries, jnp.concatenate([entering_high, entering_low], axis=0))
        tail_b = spread(tail, block, first)
        step_b = spread(step, block, first)
        skip_b = spread(skip_weight, block, first[:1])
        weighted_high, weighted_low = halves(tail_b * step_b * x)
        lifted_high, lifted_low = halves(spread(lift, block, first) * g)
        picker = jnp.where(place_lane == side + 2 * block, 1.0, 0.0).astype(BF16)
        picker = jnp.concatenate([picker, picker], axis=0)
        outward_sum = outward_sum + nn(jnp.concatenate(halves(x * message_keys), axis=1), picker)
        inward_sum = inward_sum + nn(jnp.concatenate(halves(g * state_queries), axis=1), picker)
        from_keys = from_keys + (
            nt(
                jnp.concatenate([weighted_high, weighted_low], axis=1),
                jnp.concatenate([message_high, message_high], axis=1),
            )
            + nt(weighted_high, message_low)
        )
        from_queries = from_queries + (
            nt(
                jnp.concatenate([lifted_high, lifted_low], axis=1),
                jnp.concatenate([entering_high, entering_high], axis=1),
            )
            + nt(lifted_high, entering_low)
        )
        met = jnp.sum(entering * message, axis=0, keepdims=True)
        early = jnp.sum(jnp.where(first[:1], met, 0.0), axis=1, keepdims=True)
        late = jnp.sum(jnp.where(first[:1], 0.0, met), axis=1, keepdims=True)
        meeting = jnp.where(lane_one == 2 * block, early, meeting)
        meeting = jnp.where(lane_one == 2 * block + 1, late, meeting)
        grad = step_b * (adjoint_ref[:, cols] + tail_b * message_keys) + skip_b * g
        grad_x[:, cols] = grad.astype(grad_x.dtype)
    rest[1][...] = from_keys
    rest[2][...] = from_queries
    if not final:
        rest[3][...] = outward_sum
        rest[4][...] = inward_sum
        rest[5][...] = meeting
        return
    grad_raw, sums = rest[3], rest[4]
    rate = rate_ref[...]
    inward = lift * inward_sum
    lead = tail * outward_sum
    outward = lead * step
    through = through_ref[...] + inward - outward
    last = jnp.sum(outward, axis=0, keepdims=True) + jnp.exp(closing) * meeting
    through = through + jnp.where(iota((rows, LANES), 0) == rows - 1, last, 0.0)
    upper = (iota((rows, rows), 1) >= iota((rows, rows), 0)).astype(F32)
    grad_cumulative = jnp.dot(upper, through, precision=HIGHEST, preferred_element_type=F32)
    grad_step = grad_cumulative * rate + column_ref[...] + lead
    grad_raw[...] = (grad_step * slope_ref[...]).T[:heads, :]
    rate_sum = jnp.sum(grad_cumulative * step, axis=0, keepdims=True) * rate
    sums[0:1, :] = jnp.where(lane_one < heads, rate_sum, 0.0)
    sums[1:2, :] = jnp.where(lane_one < heads, skip_ref[...], 0.0)


def combine_kernel(per, has_before, wants_send, *refs):
    refs = list(refs)
    own = refs.pop(0) if wants_send else None
    past = refs.pop(0) if has_before else None
    arrived = refs.pop(0)
    new_past = refs.pop(0) if has_before else None
    send = refs.pop(0) if wants_send else None
    tail = pl.ds(per * LANES, arrived.shape[0] - per * LANES)
    past_log = past[tail, :] if has_before else None
    new_log = arrived[tail, :] + past_log if has_before else arrived[tail, :]
    if has_before:
        new_past[tail, :] = new_log
        past_decay = jnp.exp(past_log)
    if wants_send:
        own_log = own[tail, :]
        own_decay = jnp.exp(own_log)
        send[tail, :] = own_log + new_log
    for place in range(per):
        where = pl.ds(place * LANES, LANES)
        state = arrived[where, :]
        if has_before:
            state = past[where, :] + past_decay[place : place + 1, :] * state
            new_past[where, :] = state
        if wants_send:
            send[where, :] = own[where, :] + own_decay[place : place + 1, :] * state


def chip_moves(moves, chips):
    ahead = [(2 * a + 1, 2 * b + 1) for a, b in moves]
    back = [(2 * (chips - 1 - a), 2 * (chips - 1 - b)) for a, b in moves]
    return ahead + back


ROUNDS = (
    [(z, z + 1) for z in range(0, 16, 2)],
    [(1, 3), (5, 7), (9, 11)],
    [(3, 7), (1, 2)],
    [(7, 11), (3, 5)],
    [(11, 13), (7, 9), (5, 6), (3, 4)],
    [(7, 8), (9, 10), (11, 12), (13, 14)],
)
LAST_CHIP = [(13, 15)]


def combine(per, own, past, arrived):
    shape = jax.ShapeDtypeStruct(arrived.shape, F32)
    operands = [a for a in (own, past, arrived) if a is not None]
    whole = pl.BlockSpec(memory_space=pltpu.VMEM)
    outs = (past is not None) + (own is not None)
    results = list(
        pl.pallas_call(
            functools.partial(combine_kernel, per, past is not None, own is not None),
            out_shape=[shape] * outs,
            in_specs=[whole] * len(operands),
            out_specs=[whole] * outs,
            compiler_params=pltpu.CompilerParams(vmem_limit_bytes=8 * 1024 * 1024),
            cost_estimate=pl.CostEstimate(flops=1_000_000, bytes_accessed=1_000_000, transcendentals=0),
            name="combine",
        )(*operands)
    )
    new_past = results.pop(0) if past is not None else arrived
    return new_past, (results.pop(0) if own is not None else None)


def scan_chips(keeps, pairs, per, swap, beside):
    chips = 16
    own = [combine(per, keep, None, pair)[1] for keep, pair in zip(keeps, pairs)]
    send, past = list(own), [None] * STREAMS
    for turn, moves in enumerate(ROUNDS):
        arrived = []
        for stream in range(STREAMS):
            got = [lax.ppermute(send[stream], "ctx", chip_moves(moves, chips))]
            if turn == 5:
                got.append(lax.ppermute(send[stream], "ctx", chip_moves(LAST_CHIP, chips)))
            arrived.append(got)
        if turn == 0:
            extra = beside(own)
            arrived[-1], extra = lax.optimization_barrier((arrived[-1], extra))
        for stream in range(STREAMS):
            for index, block in enumerate(arrived[stream]):
                target = own[stream] if index == 0 and turn < 5 else None
                past[stream], new_send = combine(per, target, past[stream], block)
                send[stream] = new_send if new_send is not None else send[stream]
    return past, [lax.ppermute(a, "ctx", swap) for a in past], extra


def per_device(inputs, in_keys, output_queries, step_raw, decay_log, skip_weight, grad_out):
    rows = inputs.shape[1]
    width = inputs.shape[2]
    heads = decay_log.shape[0]
    blocks = width // LANES
    per = blocks // STREAMS
    extra = (per + 7) // 8 * 8
    count = lax.axis_size("ctx")
    swap = [(i, i ^ 1) for i in range(count)]
    core = lax.rem(lax.axis_index("ctx"), 2).astype(jnp.int32).reshape(1)
    x, g, keys, queries = inputs[0], grad_out[0], in_keys[0], output_queries[0]
    raw_t = jnp.swapaxes(step_raw[0], 0, 1)
    decay_row = decay_log.reshape(1, heads)
    skip_row = skip_weight.reshape(1, heads)
    whole = pl.BlockSpec(memory_space=pltpu.VMEM)
    scalar = pl.BlockSpec(memory_space=pltpu.SMEM)
    params = pltpu.CompilerParams(vmem_limit_bytes=VMEM_LIMIT)
    tile = jax.ShapeDtypeStruct((rows, LANES), F32)
    line = jax.ShapeDtypeStruct((1, LANES), F32)
    packed = jax.ShapeDtypeStruct((per * LANES + extra, LANES), F32)
    wide = pltpu.VMEM((rows, LANES), F32)

    def fetched(a):
        return pl.BlockSpec(a.shape, lambda i: (0, 0))

    operands = (raw_t, decay_row, x, g, keys, queries)
    made = pl.pallas_call(
        functools.partial(summary_kernel, heads, blocks),
        grid=(1,),
        out_shape=[packed] * (2 * STREAMS),
        in_specs=[scalar] + [fetched(a) for a in operands],
        out_specs=[whole] * (2 * STREAMS),
        scratch_shapes=[wide],
        compiler_params=params,
        cost_estimate=pl.CostEstimate(flops=400_000_000, bytes_accessed=4_000_000, transcendentals=0),
        name="summaries",
    )(core, *operands)
    keeps, sends = made[:STREAMS], made[STREAMS:]

    def within_slab(after):
        held, _ = lax.optimization_barrier((operands, after))
        return pl.pallas_call(
            functools.partial(local_kernel, heads, blocks),
            out_shape=[jax.ShapeDtypeStruct((rows, width), F32)] + [tile] * 7 + [line] * 2,
            in_specs=[whole] * 6,
            out_specs=[whole] * 10,
            scratch_shapes=[wide, pltpu.VMEM((LANES, rows), F32)],
            compiler_params=params,
            cost_estimate=pl.CostEstimate(flops=2_000_000_000, bytes_accessed=4_000_000, transcendentals=0),
            name="within_slab",
        )(*held)

    pairs = [lax.ppermute(send, "ctx", swap) for send in sends]
    before, other, local = scan_chips(keeps, pairs, per, swap, within_slab)
    adjoint, keys_part, queries_part, *terms = local
    full = jax.ShapeDtypeStruct((rows, width), BF16)
    carried = [keys_part, queries_part]
    for stream in range(STREAMS):
        final = stream == STREAMS - 1
        shapes = [full, tile, tile]
        if final:
            shapes += [jax.ShapeDtypeStruct((heads, rows), F32), jax.ShapeDtypeStruct((2, LANES), F32)]
        else:
            shapes += [tile, tile, line]
        given = [core, skip_row, x, g, keys, queries, adjoint, *terms]
        given += [pairs[stream], before[stream], other[stream], *carried]
        done = pl.pallas_call(
            functools.partial(gradient_kernel, heads, blocks, stream),
            out_shape=shapes,
            in_specs=[scalar] + [whole] * (len(given) - 1),
            out_specs=[whole] * len(shapes),
            scratch_shapes=[pltpu.VMEM((8, LANES), F32)],
            compiler_params=params,
            cost_estimate=pl.CostEstimate(flops=800_000_000, bytes_accessed=8_000_000, transcendentals=0),
            name="gradients",
        )(*given)
        if final:
            grad_x, grad_keys, grad_queries, grad_raw_t, sums = done
        else:
            carried = [*done[1:], done[0]]
    line_sum = jnp.concatenate([sums[0, : LANES // 2], sums[1, : LANES // 2]])
    for axis in ("ctx", "dp"):
        size = lax.axis_size(axis)
        shared = jnp.broadcast_to(line_sum[None], (size, LANES))
        line_sum = jnp.sum(lax.all_to_all(shared, axis, 0, 0, tiled=True), axis=0)
    return (
        grad_x[None],
        grad_keys[None],
        grad_queries[None],
        jnp.swapaxes(grad_raw_t, 0, 1)[None],
        line_sum[:heads],
        line_sum[LANES // 2 : LANES // 2 + heads],
    )


def solution(mesh):
    placed = P("dp", "ctx", None)
    return jax.shard_map(
        per_device,
        mesh=mesh,
        in_specs=(placed, placed, placed, placed, P(), P(), placed),
        out_specs=(placed, placed, placed, placed, P(), P()),
        check_vma=False,
    )
```

```python
import functools

import jax
import jax.numpy as jnp
from jax import lax
from jax.experimental import pallas as pl
from jax.experimental.pallas import tpu as pltpu
from jax.sharding import PartitionSpec as P

F32 = jnp.float32
BF16 = jnp.bfloat16
HIGHEST = lax.Precision.HIGHEST
LANES = 128
STREAMS = 4
VMEM_LIMIT = 20 * 1024 * 1024


def nn(a, b):
    return lax.dot_general(a, b, (((1,), (0,)), ((), ())), preferred_element_type=F32)


def nt(a, b):
    return lax.dot_general(a, b, (((1,), (1,)), ((), ())), preferred_element_type=F32)


def halves(a):
    high = a.astype(BF16)
    low = (a - high.astype(F32)).astype(BF16)
    return high, low


def iota(shape, dim):
    return lax.broadcasted_iota(jnp.int32, shape, dim)


def spread(values, block, first):
    return jnp.where(first, values[:, 2 * block : 2 * block + 1], values[:, 2 * block + 1 : 2 * block + 2])


def head_terms(raw_ref, decay_ref, wide, heads):
    rows = raw_ref.shape[1]
    wide[...] = jnp.zeros_like(wide)
    wide[0:1, :heads] = decay_ref[...]
    rate = jnp.where(iota((1, LANES), 1) < heads, -jnp.exp(wide[0:1, :]), 0.0)
    wide[0:1, :] = jnp.zeros((1, LANES), F32)
    wide[:heads, :] = raw_ref[...]
    raw = wide[...].T
    step = jnp.maximum(raw, 0.0) + jnp.log1p(jnp.exp(-jnp.abs(raw)))
    lower = (iota((rows, rows), 0) >= iota((rows, rows), 1)).astype(F32)
    cumulative = jnp.dot(lower, step * rate, precision=HIGHEST, preferred_element_type=F32)
    return raw, step, rate, cumulative


def summary_kernel(heads, blocks, core_ref, *refs):
    far, refs = refs[:6], refs[6:]
    keeps, sends, near = refs[:STREAMS], refs[STREAMS], refs[STREAMS + 1 : STREAMS + 7]
    wide, arrivals = refs[STREAMS + 7], refs[STREAMS + 8]
    copies = [pltpu.make_async_copy(a, b, arrivals.at[i]) for i, (a, b) in enumerate(zip(far, near))]
    for copy in copies:
        copy.start()
    for copy in copies:
        copy.wait()
    raw_ref, decay_ref, x_ref, g_ref, b_ref, c_ref = near
    forward = core_ref[0] == 1
    raw, step, rate, cumulative = head_terms(raw_ref, decay_ref, wide, heads)
    closing = cumulative[-1:, :]
    weight = jnp.exp(closing - cumulative) * step
    lift = jnp.exp(cumulative)
    rows = cumulative.shape[0]
    first = iota((rows, LANES), 1) < LANES // 2
    keys_t = b_ref[...].astype(F32).T.astype(BF16)
    queries_t = c_ref[...].astype(F32).T.astype(BF16)
    keys_t = jnp.concatenate([keys_t, keys_t], axis=1)
    queries_t = jnp.concatenate([queries_t, queries_t], axis=1)
    per = blocks // STREAMS
    packed_rows = keeps[0].shape[0]
    for block in range(blocks):
        stream, place = block // per, block % per
        cols = pl.ds(block * LANES, LANES)
        weighted = spread(weight, block, first) * x_ref[:, cols].astype(F32)
        lifted = spread(lift, block, first) * g_ref[:, cols].astype(F32)
        state = nn(keys_t, jnp.concatenate(halves(weighted), axis=0))
        message = nn(queries_t, jnp.concatenate(halves(lifted), axis=0))
        keeps[stream][pl.ds(place * LANES, LANES), :] = jnp.where(forward, state, message)
        sends[pl.ds(stream * packed_rows + place * LANES, LANES), :] = jnp.where(forward, message, state)
    for stream in range(STREAMS):
        extra = packed_rows - per * LANES
        logs = [
            spread(closing, stream * per + place, first[:1]) for place in range(per)
        ] + [jnp.zeros((extra - per, LANES), F32)]
        logs = jnp.concatenate(logs, axis=0)
        keeps[stream][pl.ds(per * LANES, extra), :] = logs
        sends[pl.ds(stream * packed_rows + per * LANES, extra), :] = logs


def local_kernel(
    heads,
    blocks,
    raw_ref,
    decay_ref,
    x_ref,
    g_ref,
    b_ref,
    c_ref,
    adjoint_ref,
    keys_ref,
    queries_ref,
    through_ref,
    column_ref,
    step_ref,
    cumulative_ref,
    slope_ref,
    rate_ref,
    skip_ref,
    wide,
    row_t,
):
    raw, step, rate, cumulative = head_terms(raw_ref, decay_ref, wide, heads)
    rows = cumulative.shape[0]
    lane = iota((rows, LANES), 1)
    first = lane < LANES // 2
    causal = iota((rows, rows), 1) >= iota((rows, rows), 0)
    cumulative_t = cumulative.T
    keys = b_ref[...]
    queries = c_ref[...]
    scores_t = jnp.where(causal, nt(keys, queries), 0.0)
    row_t[...] = jnp.zeros_like(row_t)
    gathered = jnp.zeros((rows, rows), F32)
    column_step = jnp.zeros((rows, LANES), F32)
    skip = jnp.zeros((1, LANES), F32)
    lane_one = iota((1, LANES), 1)
    zero = jnp.zeros((rows, LANES), BF16)
    for block in range(blocks):
        cols = pl.ds(block * LANES, LANES)
        x = x_ref[:, cols]
        g = g_ref[:, cols]
        both_x = jnp.concatenate([jnp.where(first, x, zero), jnp.where(first, zero, x)], axis=0)
        both_g = jnp.concatenate([jnp.where(first, g, zero), jnp.where(first, zero, g)], axis=0)
        products = nt(both_x, g)
        highs, lows = [], []
        for half in range(2):
            head = 2 * block + half
            between = cumulative_t[head : head + 1, :] - cumulative[:, head : head + 1]
            decay = jnp.exp(jnp.minimum(between, 0.0))
            high, low = halves(decay * scores_t)
            highs.append(high)
            lows.append(low)
            scaled = decay * products[half * rows : (half + 1) * rows] * step[:, head : head + 1]
            gathered = gathered + scaled
            scored = scaled * scores_t
            row_t[head : head + 1, :] = jnp.sum(scored, axis=0, keepdims=True)
            column_step = jnp.where(lane == head, jnp.sum(scored, axis=1, keepdims=True), column_step)
        adjoint_ref[:, cols] = nn(jnp.concatenate(highs, axis=1), both_g) + nn(
            jnp.concatenate(lows, axis=1), both_g
        )
        met = jnp.sum(x.astype(F32) * g.astype(F32), axis=0, keepdims=True)
        early = jnp.sum(jnp.where(first[:1], met, 0.0), axis=1, keepdims=True)
        late = jnp.sum(jnp.where(first[:1], 0.0, met), axis=1, keepdims=True)
        skip = jnp.where(lane_one == 2 * block, early, skip)
        skip = jnp.where(lane_one == 2 * block + 1, late, skip)
    gathered = jnp.where(causal, gathered, 0.0)
    keys_ref[...] = nn(
        jnp.concatenate(halves(gathered), axis=1), jnp.concatenate([queries, queries], axis=0)
    )
    queries_ref[...] = nn(
        jnp.concatenate(halves(gathered.T), axis=1), jnp.concatenate([keys, keys], axis=0)
    )
    through_ref[...] = row_t[...].T - column_step
    column_ref[...] = column_step / step
    step_ref[...] = step
    cumulative_ref[...] = cumulative
    slope_ref[...] = 1.0 / (1.0 + jnp.exp(-raw))
    rate_ref[...] = rate
    skip_ref[...] = skip


def gradient_kernel(heads, blocks, stream, core_ref, skip_weight_ref, x_ref, g_ref, b_ref, c_ref, *rest):
    fixed, rest = rest[:9], rest[9:]
    (adjoint_ref, through_ref, column_ref, step_ref, cumulative_ref, slope_ref, rate_ref, skip_ref, pair_ref) = fixed
    before_ref, other_ref, rest = rest[0], rest[1], rest[2:]
    given = 2 if stream == 0 else 6
    taken, rest = rest[:given], rest[given:]
    final = stream == STREAMS - 1
    forward = core_ref[0] == 1
    step = step_ref[...]
    cumulative = cumulative_ref[...]
    rows = cumulative.shape[0]
    wide = rest[-1]
    wide[0:1, :] = jnp.zeros((1, LANES), F32)
    wide[0:1, :heads] = skip_weight_ref[...]
    skip_weight = wide[0:1, :]
    closing = cumulative[-1:, :]
    tail = jnp.exp(closing - cumulative)
    lift = jnp.exp(cumulative)
    first = iota((rows, LANES), 1) < LANES // 2
    lane_one = iota((1, LANES), 1)
    keys = jnp.concatenate([b_ref[...], b_ref[...]], axis=1)
    queries = jnp.concatenate([c_ref[...], c_ref[...]], axis=1)
    side = iota((LANES, LANES), 0) // (LANES // 2)
    place_lane = iota((LANES, LANES), 1)
    per = blocks // STREAMS
    from_keys = taken[0][...]
    from_queries = taken[1][...]
    if stream == 0:
        outward_sum = jnp.zeros((rows, LANES), F32)
        inward_sum = jnp.zeros((rows, LANES), F32)
        meeting = jnp.zeros((1, LANES), F32)
    else:
        outward_sum = taken[2][...]
        inward_sum = taken[3][...]
        meeting = taken[4][...]
    grad_x = rest[0]
    base = stream * before_ref.shape[0]
    if stream > 0:
        ready = pl.ds(0, stream * per * LANES)
        grad_x[:, ready] = taken[5][:, ready]
    for place in range(per):
        block = stream * per + place
        cols = pl.ds(block * LANES, LANES)
        where = pl.ds(place * LANES, LANES)
        log_row = pair_ref[pl.ds(base + per * LANES + place, 1), :]
        mine = pair_ref[pl.ds(base + place * LANES, LANES), :] + jnp.exp(log_row) * before_ref[where, :]
        theirs = other_ref[where, :]
        entering = jnp.where(forward, mine, theirs)
        message = jnp.where(forward, theirs, mine)
        entering_high, entering_low = halves(entering)
        message_high, message_low = halves(message)
        x = x_ref[:, cols].astype(F32)
        g = g_ref[:, cols].astype(F32)
        message_keys = nn(keys, jnp.concatenate([message_high, message_low], axis=0))
        state_queries = nn(queries, jnp.concatenate([entering_high, entering_low], axis=0))
        tail_b = spread(tail, block, first)
        step_b = spread(step, block, first)
        skip_b = spread(skip_weight, block, first[:1])
        weighted_high, weighted_low = halves(tail_b * step_b * x)
        lifted_high, lifted_low = halves(spread(lift, block, first) * g)
        picker = jnp.where(place_lane == side + 2 * block, 1.0, 0.0).astype(BF16)
        picker = jnp.concatenate([picker, picker], axis=0)
        outward_sum = outward_sum + nn(jnp.concatenate(halves(x * message_keys), axis=1), picker)
        inward_sum = inward_sum + nn(jnp.concatenate(halves(g * state_queries), axis=1), picker)
        from_keys = from_keys + (
            nt(
                jnp.concatenate([weighted_high, weighted_low], axis=1),
                jnp.concatenate([message_high, message_high], axis=1),
            )
            + nt(weighted_high, message_low)
        )
        from_queries = from_queries + (
            nt(
                jnp.concatenate([lifted_high, lifted_low], axis=1),
                jnp.concatenate([entering_high, entering_high], axis=1),
            )
            + nt(lifted_high, entering_low)
        )
        met = jnp.sum(entering * message, axis=0, keepdims=True)
        early = jnp.sum(jnp.where(first[:1], met, 0.0), axis=1, keepdims=True)
        late = jnp.sum(jnp.where(first[:1], 0.0, met), axis=1, keepdims=True)
        meeting = jnp.where(lane_one == 2 * block, early, meeting)
        meeting = jnp.where(lane_one == 2 * block + 1, late, meeting)
        grad = step_b * (adjoint_ref[:, cols] + tail_b * message_keys) + skip_b * g
        grad_x[:, cols] = grad.astype(grad_x.dtype)
    rest[1][...] = from_keys
    rest[2][...] = from_queries
    if not final:
        rest[3][...] = outward_sum
        rest[4][...] = inward_sum
        rest[5][...] = meeting
        return
    grad_raw, sums = rest[3], rest[4]
    rate = rate_ref[...]
    inward = lift * inward_sum
    lead = tail * outward_sum
    outward = lead * step
    through = through_ref[...] + inward - outward
    last = jnp.sum(outward, axis=0, keepdims=True) + jnp.exp(closing) * meeting
    through = through + jnp.where(iota((rows, LANES), 0) == rows - 1, last, 0.0)
    upper = (iota((rows, rows), 1) >= iota((rows, rows), 0)).astype(F32)
    grad_cumulative = jnp.dot(upper, through, precision=HIGHEST, preferred_element_type=F32)
    grad_step = grad_cumulative * rate + column_ref[...] + lead
    grad_raw[...] = (grad_step * slope_ref[...]).T[:heads, :]
    rate_sum = jnp.sum(grad_cumulative * step, axis=0, keepdims=True) * rate
    wide[0:1, :] = jnp.where(lane_one < heads, rate_sum, 0.0)
    wide[0:1, LANES // 2 :] = skip_ref[:, : LANES // 2]
    sums[...] = jnp.broadcast_to(wide[0:1, :], sums.shape)


def combine_kernel(per, base, has_before, wants_send, *refs):
    refs = list(refs)
    own = refs.pop(0) if wants_send else None
    past = refs.pop(0) if has_before else None
    arrived = refs.pop(0)
    new_past = refs.pop(0) if has_before else None
    send = refs.pop(0) if wants_send else None
    extra = (per + 7) // 8 * 8
    tail = pl.ds(per * LANES, extra)
    past_log = past[tail, :] if has_before else None
    new_log = arrived[pl.ds(base + per * LANES, extra), :]
    new_log = new_log + past_log if has_before else new_log
    if has_before:
        new_past[tail, :] = new_log
        past_decay = jnp.exp(past_log)
    if wants_send:
        own_log = own[tail, :]
        own_decay = jnp.exp(own_log)
        send[tail, :] = own_log + new_log
    for place in range(per):
        where = pl.ds(place * LANES, LANES)
        state = arrived[pl.ds(base + place * LANES, LANES), :]
        if has_before:
            state = past[where, :] + past_decay[place : place + 1, :] * state
            new_past[where, :] = state
        if wants_send:
            send[where, :] = own[where, :] + own_decay[place : place + 1, :] * state


def chip_moves(moves, chips):
    ahead = [(2 * a + 1, 2 * b + 1) for a, b in moves]
    back = [(2 * (chips - 1 - a), 2 * (chips - 1 - b)) for a, b in moves]
    return ahead + back


ROUNDS = (
    [(z, z + 1) for z in range(0, 16, 2)],
    [(1, 3), (5, 7), (9, 11)],
    [(3, 7), (1, 2)],
    [(7, 11), (3, 5)],
    [(11, 13), (7, 9), (5, 6), (3, 4)],
    [(7, 8), (9, 10), (11, 12), (13, 14)],
)
LAST_CHIP = [(13, 15)]


def combine(per, own, past, arrived, base=0):
    rows = per * LANES + (per + 7) // 8 * 8
    shape = jax.ShapeDtypeStruct((rows, LANES), F32)
    operands = [a for a in (own, past, arrived) if a is not None]
    whole = pl.BlockSpec(memory_space=pltpu.VMEM)
    outs = (past is not None) + (own is not None)
    results = list(
        pl.pallas_call(
            functools.partial(combine_kernel, per, base, past is not None, own is not None),
            out_shape=[shape] * outs,
            in_specs=[whole] * len(operands),
            out_specs=[whole] * outs,
            compiler_params=pltpu.CompilerParams(vmem_limit_bytes=8 * 1024 * 1024),
            cost_estimate=pl.CostEstimate(flops=1_000_000, bytes_accessed=1_000_000, transcendentals=0),
            name="combine",
        )(*operands)
    )
    new_past = results.pop(0) if past is not None else arrived
    return new_past, (results.pop(0) if own is not None else None)


def scan_chips(keeps, pair, per, swap, within, gradients):
    chips = 16
    rows = keeps[0].shape[0]
    own = [combine(per, keep, None, pair, i * rows)[1] for i, keep in enumerate(keeps)]
    send, past = list(own), [None] * STREAMS
    final = len(ROUNDS) - 1
    for turn, moves in enumerate(ROUNDS):
        arrived = []
        for stream in range(STREAMS):
            got = [lax.ppermute(send[stream], "ctx", chip_moves(moves, chips))]
            if turn == final:
                got.append(lax.ppermute(send[stream], "ctx", chip_moves(LAST_CHIP, chips)))
            arrived.append(got)
        if turn == final:
            local = within(send[-1])
            carried = None
        for stream in range(STREAMS):
            if turn == final and stream == STREAMS - 1 and stream > 0:
                arrived[stream], carried = lax.optimization_barrier((arrived[stream], carried))
            for block in arrived[stream]:
                target = own[stream] if turn < final else None
                past[stream], new_send = combine(per, target, past[stream], block)
                send[stream] = new_send if new_send is not None else send[stream]
            if turn == final:
                other = lax.ppermute(past[stream], "ctx", swap)
                carried = gradients(stream, local, past[stream], other, carried)
    return carried


def per_device(inputs, in_keys, output_queries, step_raw, decay_log, skip_weight, grad_out):
    rows = inputs.shape[1]
    width = inputs.shape[2]
    heads = decay_log.shape[0]
    blocks = width // LANES
    per = blocks // STREAMS
    extra = (per + 7) // 8 * 8
    count = lax.axis_size("ctx")
    swap = [(i, i ^ 1) for i in range(count)]
    core = lax.rem(lax.axis_index("ctx"), 2).astype(jnp.int32).reshape(1)
    x, g, keys, queries = inputs[0], grad_out[0], in_keys[0], output_queries[0]
    raw_t = jnp.swapaxes(step_raw[0], 0, 1)
    decay_row = decay_log.reshape(1, heads)
    skip_row = skip_weight.reshape(1, heads)
    whole = pl.BlockSpec(memory_space=pltpu.VMEM)
    scalar = pl.BlockSpec(memory_space=pltpu.SMEM)
    params = pltpu.CompilerParams(vmem_limit_bytes=VMEM_LIMIT)
    tile = jax.ShapeDtypeStruct((rows, LANES), F32)
    line = jax.ShapeDtypeStruct((1, LANES), F32)
    packed = jax.ShapeDtypeStruct((per * LANES + extra, LANES), F32)
    wide = pltpu.VMEM((rows, LANES), F32)

    operands = (raw_t, decay_row, x, g, keys, queries)
    far = pl.BlockSpec(memory_space=pltpu.HBM)
    made = pl.pallas_call(
        functools.partial(summary_kernel, heads, blocks),
        out_shape=[packed] * STREAMS + [jax.ShapeDtypeStruct((STREAMS * packed.shape[0], LANES), F32)],
        in_specs=[scalar] + [far] * 6,
        out_specs=[whole] * (STREAMS + 1),
        scratch_shapes=[pltpu.VMEM(a.shape, a.dtype) for a in operands]
        + [wide, pltpu.SemaphoreType.DMA((6,))],
        compiler_params=params,
        cost_estimate=pl.CostEstimate(flops=400_000_000, bytes_accessed=4_000_000, transcendentals=0),
        name="summaries",
    )(core, *operands)
    keeps, sends = made[:STREAMS], made[STREAMS]

    def within_slab(after):
        held, _ = lax.optimization_barrier((operands, after))
        return pl.pallas_call(
            functools.partial(local_kernel, heads, blocks),
            out_shape=[jax.ShapeDtypeStruct((rows, width), F32)] + [tile] * 7 + [line] * 2,
            in_specs=[whole] * 6,
            out_specs=[whole] * 10,
            scratch_shapes=[wide, pltpu.VMEM((LANES, rows), F32)],
            compiler_params=params,
            cost_estimate=pl.CostEstimate(flops=2_000_000_000, bytes_accessed=4_000_000, transcendentals=0),
            name="within_slab",
        )(*held)

    full = jax.ShapeDtypeStruct((rows, width), BF16)

    def gradients(stream, local, before, other, carried):
        final = stream == STREAMS - 1
        shapes = [full, tile, tile]
        if final:
            shapes += [jax.ShapeDtypeStruct((heads, rows), F32), jax.ShapeDtypeStruct((count, LANES), F32)]
        else:
            shapes += [tile, tile, line]
        adjoint, keys_part, queries_part, *terms = local
        carried = [keys_part, queries_part] if carried is None else [*carried[1:], carried[0]]
        given = [core, skip_row, x, g, keys, queries, adjoint, *terms, pair, before, other, *carried]
        return pl.pallas_call(
            functools.partial(gradient_kernel, heads, blocks, stream),
            out_shape=shapes,
            in_specs=[scalar] + [whole] * (len(given) - 1),
            out_specs=[whole] * len(shapes),
            scratch_shapes=[pltpu.VMEM((8, LANES), F32)],
            compiler_params=params,
            cost_estimate=pl.CostEstimate(flops=800_000_000, bytes_accessed=8_000_000, transcendentals=0),
            name="gradients",
        )(*given)

    pair = lax.ppermute(sends, "ctx", swap)
    done = scan_chips(keeps, pair, per, swap, within_slab, gradients)
    grad_x, grad_keys, grad_queries, grad_raw_t, shared = done
    shared = lax.all_to_all(shared, "ctx", 0, 0, tiled=True)
    line_sum = jnp.sum(shared, axis=0)
    shared = jnp.broadcast_to(line_sum[None], (lax.axis_size("dp"), LANES))
    line_sum = jnp.sum(lax.all_to_all(shared, "dp", 0, 0, tiled=True), axis=0)
    return (
        grad_x[None],
        grad_keys[None],
        grad_queries[None],
        jnp.swapaxes(grad_raw_t, 0, 1)[None],
        line_sum[:heads],
        line_sum[LANES // 2 : LANES // 2 + heads],
    )


def solution(mesh):
    placed = P("dp", "ctx", None)
    return jax.shard_map(
        per_device,
        mesh=mesh,
        in_specs=(placed, placed, placed, placed, P(), P(), placed),
        out_specs=(placed, placed, placed, placed, P(), P()),
        check_vma=False,
    )
```

```python
import functools

import jax
import jax.numpy as jnp
from jax import lax
from jax.experimental import pallas as pl
from jax.experimental.pallas import tpu as pltpu
from jax.sharding import PartitionSpec as P

F32 = jnp.float32
BF16 = jnp.bfloat16
HIGHEST = lax.Precision.HIGHEST
LANES = 128
SIZES = (5, 5, 5, 5)
STREAMS = len(SIZES)
STARTS = tuple(sum(SIZES[:i]) for i in range(STREAMS))
LOG_ROWS = 8
ROWS = tuple(size * LANES + LOG_ROWS for size in SIZES)
BASES = tuple(sum(ROWS[:i]) for i in range(STREAMS))
VMEM_LIMIT = 20 * 1024 * 1024


def nn(a, b):
    return lax.dot_general(a, b, (((1,), (0,)), ((), ())), preferred_element_type=F32)


def nt(a, b):
    return lax.dot_general(a, b, (((1,), (1,)), ((), ())), preferred_element_type=F32)


def halves(a):
    high = a.astype(BF16)
    low = (a - high.astype(F32)).astype(BF16)
    return high, low


def iota(shape, dim):
    return lax.broadcasted_iota(jnp.int32, shape, dim)


def spread(values, block, first):
    return jnp.where(first, values[:, 2 * block : 2 * block + 1], values[:, 2 * block + 1 : 2 * block + 2])


def head_terms(raw_ref, decay_ref, wide, heads):
    rows = raw_ref.shape[1]
    wide[...] = jnp.zeros_like(wide)
    wide[0:1, :heads] = decay_ref[...]
    rate = jnp.where(iota((1, LANES), 1) < heads, -jnp.exp(wide[0:1, :]), 0.0)
    wide[0:1, :] = jnp.zeros((1, LANES), F32)
    wide[:heads, :] = raw_ref[...]
    raw = wide[...].T
    step = jnp.maximum(raw, 0.0) + jnp.log1p(jnp.exp(-jnp.abs(raw)))
    lower = (iota((rows, rows), 0) >= iota((rows, rows), 1)).astype(F32)
    cumulative = jnp.dot(lower, step * rate, precision=HIGHEST, preferred_element_type=F32)
    return raw, step, rate, cumulative


def summary_kernel(heads, blocks, core_ref, *refs):
    far, refs = refs[:6], refs[6:]
    keeps, sends, near = refs[:STREAMS], refs[STREAMS], refs[STREAMS + 1 : STREAMS + 7]
    wide, arrivals = refs[STREAMS + 7], refs[STREAMS + 8]
    copies = [pltpu.make_async_copy(a, b, arrivals.at[i]) for i, (a, b) in enumerate(zip(far, near))]
    for copy in copies:
        copy.start()
    for copy in copies:
        copy.wait()
    raw_ref, decay_ref, x_ref, g_ref, b_ref, c_ref = near
    forward = core_ref[0] == 1
    raw, step, rate, cumulative = head_terms(raw_ref, decay_ref, wide, heads)
    closing = cumulative[-1:, :]
    weight = jnp.exp(closing - cumulative) * step
    lift = jnp.exp(cumulative)
    rows = cumulative.shape[0]
    first = iota((rows, LANES), 1) < LANES // 2
    keys_t = b_ref[...].astype(F32).T.astype(BF16)
    queries_t = c_ref[...].astype(F32).T.astype(BF16)
    keys_t = jnp.concatenate([keys_t, keys_t], axis=1)
    queries_t = jnp.concatenate([queries_t, queries_t], axis=1)
    for stream, place in [(i, j) for i in range(STREAMS) for j in range(SIZES[i])]:
        block = STARTS[stream] + place
        cols = pl.ds(block * LANES, LANES)
        weighted = spread(weight, block, first) * x_ref[:, cols].astype(F32)
        lifted = spread(lift, block, first) * g_ref[:, cols].astype(F32)
        state = nn(keys_t, jnp.concatenate(halves(weighted), axis=0))
        message = nn(queries_t, jnp.concatenate(halves(lifted), axis=0))
        keeps[stream][pl.ds(place * LANES, LANES), :] = jnp.where(forward, state, message)
        sends[pl.ds(BASES[stream] + place * LANES, LANES), :] = jnp.where(forward, message, state)
    for stream in range(STREAMS):
        size = SIZES[stream]
        logs = [spread(closing, STARTS[stream] + place, first[:1]) for place in range(size)]
        logs = jnp.concatenate(logs + [jnp.zeros((LOG_ROWS - size, LANES), F32)], axis=0)
        keeps[stream][pl.ds(size * LANES, LOG_ROWS), :] = logs
        sends[pl.ds(BASES[stream] + size * LANES, LOG_ROWS), :] = logs


def local_kernel(heads, blocks, part, *refs):
    start, stop = (0, SIZES[0]) if part == 0 else (SIZES[0], blocks)
    if part == 0:
        raw_ref, decay_ref, x_ref, g_ref, b_ref, c_ref = refs[:6]
        outs, (wide, row_t) = refs[6:15], refs[15:]
        raw, step, rate, cumulative = head_terms(raw_ref, decay_ref, wide, heads)
    else:
        x_ref, g_ref, b_ref, c_ref = refs[:4]
        gathered_in, row_in, column_in, skip_in, step_ref, cumulative_ref = refs[4:10]
        outs, (row_t,) = refs[10:16], refs[16:]
        step = step_ref[...]
        cumulative = cumulative_ref[...]
    rows = cumulative.shape[0]
    lane = iota((rows, LANES), 1)
    first = lane < LANES // 2
    causal = iota((rows, rows), 1) >= iota((rows, rows), 0)
    cumulative_t = cumulative.T
    keys = b_ref[...]
    queries = c_ref[...]
    scores_t = jnp.where(causal, nt(keys, queries), 0.0)
    lane_one = iota((1, LANES), 1)
    zero = jnp.zeros((rows, LANES), BF16)
    if part == 0:
        row_t[...] = jnp.zeros_like(row_t)
        gathered = jnp.zeros((rows, rows), F32)
        column_step = jnp.zeros((rows, LANES), F32)
        skip = jnp.zeros((1, LANES), F32)
    else:
        row_t[...] = row_in[...]
        gathered = gathered_in[...]
        column_step = column_in[...]
        skip = skip_in[...]
    for block in range(start, stop):
        place = block - start
        cols = pl.ds(block * LANES, LANES)
        x = x_ref[:, cols]
        g = g_ref[:, cols]
        both_x = jnp.concatenate([jnp.where(first, x, zero), jnp.where(first, zero, x)], axis=0)
        both_g = jnp.concatenate([jnp.where(first, g, zero), jnp.where(first, zero, g)], axis=0)
        products = nt(both_x, g)
        highs, lows = [], []
        for side in range(2):
            head = 2 * block + side
            between = cumulative_t[head : head + 1, :] - cumulative[:, head : head + 1]
            decay = jnp.exp(jnp.minimum(between, 0.0))
            high, low = halves(decay * scores_t)
            highs.append(high)
            lows.append(low)
            scaled = decay * products[side * rows : (side + 1) * rows] * step[:, head : head + 1]
            gathered = gathered + scaled
            scored = scaled * scores_t
            row_t[head : head + 1, :] = jnp.sum(scored, axis=0, keepdims=True)
            column_step = jnp.where(lane == head, jnp.sum(scored, axis=1, keepdims=True), column_step)
        outs[0][:, pl.ds(place * LANES, LANES)] = nn(jnp.concatenate(highs, axis=1), both_g) + nn(
            jnp.concatenate(lows, axis=1), both_g
        )
        met = jnp.sum(x.astype(F32) * g.astype(F32), axis=0, keepdims=True)
        early = jnp.sum(jnp.where(first[:1], met, 0.0), axis=1, keepdims=True)
        late = jnp.sum(jnp.where(first[:1], 0.0, met), axis=1, keepdims=True)
        skip = jnp.where(lane_one == 2 * block, early, skip)
        skip = jnp.where(lane_one == 2 * block + 1, late, skip)
    if part == 0:
        values = (gathered, row_t[...], column_step, skip, step, cumulative, 1.0 / (1.0 + jnp.exp(-raw)), rate)
    else:
        gathered = jnp.where(causal, gathered, 0.0)
        values = (
            nn(jnp.concatenate(halves(gathered), axis=1), jnp.concatenate([queries, queries], axis=0)),
            nn(jnp.concatenate(halves(gathered.T), axis=1), jnp.concatenate([keys, keys], axis=0)),
            row_t[...].T - column_step,
            column_step / step,
            skip,
        )
    for out, value in zip(outs[1:], values):
        out[...] = value


def gradient_kernel(heads, blocks, stream, core_ref, skip_weight_ref, x_ref, g_ref, b_ref, c_ref, *rest):
    fixed, rest = rest[:9], rest[9:]
    (adjoint_ref, through_ref, column_ref, step_ref, cumulative_ref, slope_ref, rate_ref, skip_ref, pair_ref) = fixed
    before_ref, other_ref, rest = rest[0], rest[1], rest[2:]
    given = 2 if stream == 0 else 6
    taken, rest = rest[:given], rest[given:]
    final = stream == STREAMS - 1
    forward = core_ref[0] == 1
    step = step_ref[...]
    cumulative = cumulative_ref[...]
    rows = cumulative.shape[0]
    wide = rest[-1]
    wide[0:1, :] = jnp.zeros((1, LANES), F32)
    wide[0:1, :heads] = skip_weight_ref[...]
    skip_weight = wide[0:1, :]
    closing = cumulative[-1:, :]
    tail = jnp.exp(closing - cumulative)
    lift = jnp.exp(cumulative)
    first = iota((rows, LANES), 1) < LANES // 2
    lane_one = iota((1, LANES), 1)
    keys = jnp.concatenate([b_ref[...], b_ref[...]], axis=1)
    queries = jnp.concatenate([c_ref[...], c_ref[...]], axis=1)
    side = iota((LANES, LANES), 0) // (LANES // 2)
    place_lane = iota((LANES, LANES), 1)
    from_keys = taken[0][...]
    from_queries = taken[1][...]
    if stream == 0:
        outward_sum = jnp.zeros((rows, LANES), F32)
        inward_sum = jnp.zeros((rows, LANES), F32)
        meeting = jnp.zeros((1, LANES), F32)
    else:
        outward_sum = taken[2][...]
        inward_sum = taken[3][...]
        meeting = taken[4][...]
    grad_x = rest[0]
    base, size, start = BASES[stream], SIZES[stream], STARTS[stream]
    if stream > 0:
        ready = pl.ds(0, start * LANES)
        grad_x[:, ready] = taken[5][:, ready]
    for place in range(size):
        block = start + place
        cols = pl.ds(block * LANES, LANES)
        where = pl.ds(place * LANES, LANES)
        log_row = pair_ref[pl.ds(base + size * LANES + place, 1), :]
        mine = pair_ref[pl.ds(base + place * LANES, LANES), :] + jnp.exp(log_row) * before_ref[where, :]
        theirs = other_ref[where, :]
        entering = jnp.where(forward, mine, theirs)
        message = jnp.where(forward, theirs, mine)
        entering_high, entering_low = halves(entering)
        message_high, message_low = halves(message)
        x = x_ref[:, cols].astype(F32)
        g = g_ref[:, cols].astype(F32)
        message_keys = nn(keys, jnp.concatenate([message_high, message_low], axis=0))
        state_queries = nn(queries, jnp.concatenate([entering_high, entering_low], axis=0))
        tail_b = spread(tail, block, first)
        step_b = spread(step, block, first)
        skip_b = spread(skip_weight, block, first[:1])
        weighted_high, weighted_low = halves(tail_b * step_b * x)
        lifted_high, lifted_low = halves(spread(lift, block, first) * g)
        picker = jnp.where(place_lane == side + 2 * block, 1.0, 0.0).astype(BF16)
        picker = jnp.concatenate([picker, picker], axis=0)
        outward_sum = outward_sum + nn(jnp.concatenate(halves(x * message_keys), axis=1), picker)
        inward_sum = inward_sum + nn(jnp.concatenate(halves(g * state_queries), axis=1), picker)
        from_keys = from_keys + (
            nt(
                jnp.concatenate([weighted_high, weighted_low], axis=1),
                jnp.concatenate([message_high, message_high], axis=1),
            )
            + nt(weighted_high, message_low)
        )
        from_queries = from_queries + (
            nt(
                jnp.concatenate([lifted_high, lifted_low], axis=1),
                jnp.concatenate([entering_high, entering_high], axis=1),
            )
            + nt(lifted_high, entering_low)
        )
        met = jnp.sum(entering * message, axis=0, keepdims=True)
        early = jnp.sum(jnp.where(first[:1], met, 0.0), axis=1, keepdims=True)
        late = jnp.sum(jnp.where(first[:1], 0.0, met), axis=1, keepdims=True)
        meeting = jnp.where(lane_one == 2 * block, early, meeting)
        meeting = jnp.where(lane_one == 2 * block + 1, late, meeting)
        near = pl.ds((block if stream == 0 else block - SIZES[0]) * LANES, LANES)
        grad = step_b * (adjoint_ref[:, near] + tail_b * message_keys) + skip_b * g
        grad_x[:, cols] = grad.astype(grad_x.dtype)
    rest[1][...] = from_keys
    rest[2][...] = from_queries
    if not final:
        rest[3][...] = outward_sum
        rest[4][...] = inward_sum
        rest[5][...] = meeting
        return
    grad_raw, sums = rest[3], rest[4]
    rate = rate_ref[...]
    inward = lift * inward_sum
    lead = tail * outward_sum
    outward = lead * step
    through = through_ref[...] + inward - outward
    last = jnp.sum(outward, axis=0, keepdims=True) + jnp.exp(closing) * meeting
    through = through + jnp.where(iota((rows, LANES), 0) == rows - 1, last, 0.0)
    upper = (iota((rows, rows), 1) >= iota((rows, rows), 0)).astype(F32)
    grad_cumulative = jnp.dot(upper, through, precision=HIGHEST, preferred_element_type=F32)
    grad_step = grad_cumulative * rate + column_ref[...] + lead
    grad_raw[...] = (grad_step * slope_ref[...]).T[:heads, :]
    rate_sum = jnp.sum(grad_cumulative * step, axis=0, keepdims=True) * rate
    wide[0:1, :] = jnp.where(lane_one < heads, rate_sum, 0.0)
    wide[0:1, LANES // 2 :] = skip_ref[:, : LANES // 2]
    sums[...] = jnp.broadcast_to(wide[0:1, :], sums.shape)


def combine_kernel(size, has_before, wants_send, *refs):
    refs = list(refs)
    own = refs.pop(0) if wants_send else None
    past = refs.pop(0) if has_before else None
    arrived = refs.pop(0)
    new_past = refs.pop(0) if has_before else None
    send = refs.pop(0) if wants_send else None
    tail = pl.ds(size * LANES, LOG_ROWS)
    past_log = past[tail, :] if has_before else None
    new_log = arrived[tail, :] + past_log if has_before else arrived[tail, :]
    if has_before:
        new_past[tail, :] = new_log
        past_decay = jnp.exp(past_log)
    if wants_send:
        own_log = own[tail, :]
        own_decay = jnp.exp(own_log)
        send[tail, :] = own_log + new_log
    for place in range(size):
        where = pl.ds(place * LANES, LANES)
        state = arrived[where, :]
        if has_before:
            state = past[where, :] + past_decay[place : place + 1, :] * state
            new_past[where, :] = state
        if wants_send:
            send[where, :] = own[where, :] + own_decay[place : place + 1, :] * state


def chip_moves(moves, chips):
    ahead = [(2 * a + 1, 2 * b + 1) for a, b in moves]
    back = [(2 * (chips - 1 - a), 2 * (chips - 1 - b)) for a, b in moves]
    return ahead + back


ROUNDS = (
    [(z, z + 1) for z in range(0, 16, 2)],
    [(1, 3), (5, 7), (9, 11)],
    [(3, 7), (1, 2)],
    [(7, 11), (3, 5)],
    [(11, 13), (7, 9), (5, 6), (3, 4)],
    [(7, 8), (9, 10), (11, 12), (13, 14)],
)
LAST_CHIP = [(13, 15)]


def combine(size, own, past, arrived):
    shape = jax.ShapeDtypeStruct(arrived.shape, F32)
    operands = [a for a in (own, past, arrived) if a is not None]
    whole = pl.BlockSpec(memory_space=pltpu.VMEM)
    outs = (past is not None) + (own is not None)
    results = list(
        pl.pallas_call(
            functools.partial(combine_kernel, size, past is not None, own is not None),
            out_shape=[shape] * outs,
            in_specs=[whole] * len(operands),
            out_specs=[whole] * outs,
            compiler_params=pltpu.CompilerParams(vmem_limit_bytes=8 * 1024 * 1024),
            cost_estimate=pl.CostEstimate(flops=1_000_000, bytes_accessed=1_000_000, transcendentals=0),
            name="combine",
        )(*operands)
    )
    new_past = results.pop(0) if past is not None else arrived
    return new_past, (results.pop(0) if own is not None else None)


def first_kernel(*refs):
    keeps, pair, owns = refs[:STREAMS], refs[STREAMS], refs[STREAMS + 1 :]
    for keep, own, base, size in zip(keeps, owns, BASES, SIZES):
        tail = pl.ds(size * LANES, LOG_ROWS)
        log = keep[tail, :]
        decay = jnp.exp(log)
        own[tail, :] = log + pair[pl.ds(base + size * LANES, LOG_ROWS), :]
        for place in range(size):
            where = pl.ds(place * LANES, LANES)
            own[where, :] = keep[where, :] + decay[place : place + 1, :] * pair[pl.ds(base + place * LANES, LANES), :]


def scan_chips(keeps, pair, swap, within, gradients):
    chips = 16
    whole = pl.BlockSpec(memory_space=pltpu.VMEM)
    own = pl.pallas_call(
        first_kernel,
        out_shape=[jax.ShapeDtypeStruct(keep.shape, F32) for keep in keeps],
        in_specs=[whole] * (STREAMS + 1),
        out_specs=[whole] * STREAMS,
        compiler_params=pltpu.CompilerParams(vmem_limit_bytes=8 * 1024 * 1024),
        cost_estimate=pl.CostEstimate(flops=1_000_000, bytes_accessed=4_000_000, transcendentals=0),
        name="pair_up",
    )(*keeps, pair)
    send, past = list(own), [None] * STREAMS
    final = len(ROUNDS) - 1
    carried = None
    for turn, moves in enumerate(ROUNDS):
        arrived = []
        for stream in range(STREAMS):
            got = [lax.ppermute(send[stream], "ctx", chip_moves(moves, chips))]
            if turn == final:
                got.append(lax.ppermute(send[stream], "ctx", chip_moves(LAST_CHIP, chips)))
            arrived.append(got)
        if turn == 0:
            local = within(own[-1])
            arrived[0], local = lax.optimization_barrier((arrived[0], local))
        if turn > 0:
            arrived[0], _ = lax.optimization_barrier((arrived[0], previous))
        previous = arrived[-1]
        for stream in range(STREAMS):
            if turn == final and stream == STREAMS - 1 and stream > 0:
                arrived[stream], carried = lax.optimization_barrier((arrived[stream], carried))
            for block in arrived[stream]:
                target = own[stream] if turn < final else None
                past[stream], new_send = combine(SIZES[stream], target, past[stream], block)
                send[stream] = new_send if new_send is not None else send[stream]
            if turn == final:
                other = lax.ppermute(past[stream], "ctx", swap)
                carried = gradients(stream, local, past[stream], other, carried)
    return carried


def per_device(inputs, in_keys, output_queries, step_raw, decay_log, skip_weight, grad_out):
    rows = inputs.shape[1]
    width = inputs.shape[2]
    heads = decay_log.shape[0]
    blocks = width // LANES
    count = lax.axis_size("ctx")
    swap = [(i, i ^ 1) for i in range(count)]
    core = lax.rem(lax.axis_index("ctx"), 2).astype(jnp.int32).reshape(1)
    x, g, keys, queries = inputs[0], grad_out[0], in_keys[0], output_queries[0]
    raw_t = jnp.swapaxes(step_raw[0], 0, 1)
    decay_row = decay_log.reshape(1, heads)
    skip_row = skip_weight.reshape(1, heads)
    whole = pl.BlockSpec(memory_space=pltpu.VMEM)
    scalar = pl.BlockSpec(memory_space=pltpu.SMEM)
    params = pltpu.CompilerParams(vmem_limit_bytes=VMEM_LIMIT)
    tile = jax.ShapeDtypeStruct((rows, LANES), F32)
    line = jax.ShapeDtypeStruct((1, LANES), F32)
    packed = [jax.ShapeDtypeStruct((count_rows, LANES), F32) for count_rows in (*ROWS, sum(ROWS))]
    wide = pltpu.VMEM((rows, LANES), F32)

    operands = (raw_t, decay_row, x, g, keys, queries)
    far = pl.BlockSpec(memory_space=pltpu.HBM)
    made = pl.pallas_call(
        functools.partial(summary_kernel, heads, blocks),
        out_shape=packed,
        in_specs=[scalar] + [far] * 6,
        out_specs=[whole] * (STREAMS + 1),
        scratch_shapes=[pltpu.VMEM(a.shape, a.dtype) for a in operands]
        + [wide, pltpu.SemaphoreType.DMA((6,))],
        compiler_params=params,
        cost_estimate=pl.CostEstimate(flops=400_000_000, bytes_accessed=4_000_000, transcendentals=0),
        name="summaries",
    )(core, *operands)
    keeps, sends = made[:STREAMS], made[STREAMS]

    parts = [jax.ShapeDtypeStruct((rows, n * LANES), F32) for n in (SIZES[0], blocks - SIZES[0])]
    row_scratch = pltpu.VMEM((LANES, rows), F32)

    def local_part(part, held, out_shape, scratch):
        return pl.pallas_call(
            functools.partial(local_kernel, heads, blocks, part),
            out_shape=out_shape,
            in_specs=[whole] * len(held),
            out_specs=[whole] * len(out_shape),
            scratch_shapes=scratch,
            compiler_params=params,
            cost_estimate=pl.CostEstimate(flops=1_000_000_000, bytes_accessed=3_000_000, transcendentals=0),
            name="within_slab",
        )(*held)

    held, keeps = lax.optimization_barrier((operands, keeps))
    pair = lax.ppermute(sends, "ctx", swap)
    early = local_part(0, held, [parts[0]] + [tile] * 3 + [line] + [tile] * 3 + [line], [wide, row_scratch])
    pair, early = lax.optimization_barrier((pair, early))

    def within_slab(after):
        again, _ = lax.optimization_barrier(((*operands[2:], *early[1:7]), after))
        late = local_part(1, again, [parts[1]] + [tile] * 4 + [line], [row_scratch])
        return [early[0], late[0], *late[1:5], *early[5:9], late[5]]

    full = jax.ShapeDtypeStruct((rows, width), BF16)

    def gradients(stream, local, before, other, carried):
        final = stream == STREAMS - 1
        shapes = [full, tile, tile]
        if final:
            shapes += [jax.ShapeDtypeStruct((heads, rows), F32), jax.ShapeDtypeStruct((count, LANES), F32)]
        else:
            shapes += [tile, tile, line]
        adjoint = local[0] if stream == 0 else local[1]
        keys_part, queries_part, *terms = local[2:]
        carried = [keys_part, queries_part] if carried is None else [*carried[1:], carried[0]]
        given = [core, skip_row, x, g, keys, queries, adjoint, *terms, pair, before, other, *carried]
        return pl.pallas_call(
            functools.partial(gradient_kernel, heads, blocks, stream),
            out_shape=shapes,
            in_specs=[scalar] + [whole] * (len(given) - 1),
            out_specs=[whole] * len(shapes),
            scratch_shapes=[pltpu.VMEM((8, LANES), F32)],
            compiler_params=params,
            cost_estimate=pl.CostEstimate(flops=800_000_000, bytes_accessed=8_000_000, transcendentals=0),
            name="gradients",
        )(*given)

    done = scan_chips(keeps, pair, swap, within_slab, gradients)
    grad_x, grad_keys, grad_queries, grad_raw_t, shared = done
    shared = lax.all_to_all(shared, "ctx", 0, 0, tiled=True)
    line_sum = jnp.sum(shared, axis=0)
    shared = jnp.broadcast_to(line_sum[None], (lax.axis_size("dp"), LANES))
    line_sum = jnp.sum(lax.all_to_all(shared, "dp", 0, 0, tiled=True), axis=0)
    return (
        grad_x[None],
        grad_keys[None],
        grad_queries[None],
        jnp.swapaxes(grad_raw_t, 0, 1)[None],
        line_sum[:heads],
        line_sum[LANES // 2 : LANES // 2 + heads],
    )


def solution(mesh):
    placed = P("dp", "ctx", None)
    return jax.shard_map(
        per_device,
        mesh=mesh,
        in_specs=(placed, placed, placed, placed, P(), P(), placed),
        out_specs=(placed, placed, placed, placed, P(), P()),
        check_vma=False,
    )
```

```python
import functools

import jax
import jax.numpy as jnp
from jax import lax
from jax.experimental import pallas as pl
from jax.experimental.pallas import tpu as pltpu
from jax.sharding import PartitionSpec as P

F32 = jnp.float32
BF16 = jnp.bfloat16
HIGHEST = lax.Precision.HIGHEST
LANES = 128
SIZES = (5, 5, 5, 5)
STREAMS = len(SIZES)
STARTS = tuple(sum(SIZES[:i]) for i in range(STREAMS))
LOG_ROWS = 8
ROWS = tuple(size * LANES + LOG_ROWS for size in SIZES)
BASES = tuple(sum(ROWS[:i]) for i in range(STREAMS))
VMEM_LIMIT = 20 * 1024 * 1024


def nn(a, b):
    return lax.dot_general(a, b, (((1,), (0,)), ((), ())), preferred_element_type=F32)


def nt(a, b):
    return lax.dot_general(a, b, (((1,), (1,)), ((), ())), preferred_element_type=F32)


def halves(a):
    high = a.astype(BF16)
    low = (a - high.astype(F32)).astype(BF16)
    return high, low


def iota(shape, dim):
    return lax.broadcasted_iota(jnp.int32, shape, dim)


def spread(values, block, first):
    return jnp.where(first, values[:, 2 * block : 2 * block + 1], values[:, 2 * block + 1 : 2 * block + 2])


def head_terms(raw_ref, decay_ref, wide, heads):
    rows = raw_ref.shape[1]
    wide[...] = jnp.zeros_like(wide)
    wide[0:1, :heads] = decay_ref[...]
    rate = jnp.where(iota((1, LANES), 1) < heads, -jnp.exp(wide[0:1, :]), 0.0)
    wide[0:1, :] = jnp.zeros((1, LANES), F32)
    wide[:heads, :] = raw_ref[...]
    raw = wide[...].T
    step = jnp.maximum(raw, 0.0) + jnp.log1p(jnp.exp(-jnp.abs(raw)))
    lower = (iota((rows, rows), 0) >= iota((rows, rows), 1)).astype(F32)
    cumulative = jnp.dot(lower, step * rate, precision=HIGHEST, preferred_element_type=F32)
    return raw, step, rate, cumulative


def summary_kernel(heads, blocks, core_ref, *refs):
    far, refs = refs[:6], refs[6:]
    keeps, sends, near = refs[:STREAMS], refs[STREAMS], refs[STREAMS + 1 : STREAMS + 7]
    wide, arrivals = refs[STREAMS + 7], refs[STREAMS + 8]
    copies = [pltpu.make_async_copy(a, b, arrivals.at[i]) for i, (a, b) in enumerate(zip(far, near))]
    for copy in copies:
        copy.start()
    for copy in copies:
        copy.wait()
    raw_ref, decay_ref, x_ref, g_ref, b_ref, c_ref = near
    forward = core_ref[0] == 1
    raw, step, rate, cumulative = head_terms(raw_ref, decay_ref, wide, heads)
    closing = cumulative[-1:, :]
    weight = jnp.exp(closing - cumulative) * step
    lift = jnp.exp(cumulative)
    rows = cumulative.shape[0]
    first = iota((rows, LANES), 1) < LANES // 2
    keys_t = b_ref[...].astype(F32).T.astype(BF16)
    queries_t = c_ref[...].astype(F32).T.astype(BF16)
    keys_t = jnp.concatenate([keys_t, keys_t], axis=1)
    queries_t = jnp.concatenate([queries_t, queries_t], axis=1)
    for stream, place in [(i, j) for i in range(STREAMS) for j in range(SIZES[i])]:
        block = STARTS[stream] + place
        cols = pl.ds(block * LANES, LANES)
        weighted = spread(weight, block, first) * x_ref[:, cols].astype(F32)
        lifted = spread(lift, block, first) * g_ref[:, cols].astype(F32)
        state = nn(keys_t, jnp.concatenate(halves(weighted), axis=0))
        message = nn(queries_t, jnp.concatenate(halves(lifted), axis=0))
        keeps[stream][pl.ds(place * LANES, LANES), :] = jnp.where(forward, state, message)
        sends[pl.ds(BASES[stream] + place * LANES, LANES), :] = jnp.where(forward, message, state)
    for stream in range(STREAMS):
        size = SIZES[stream]
        logs = [spread(closing, STARTS[stream] + place, first[:1]) for place in range(size)]
        logs = jnp.concatenate(logs + [jnp.zeros((LOG_ROWS - size, LANES), F32)], axis=0)
        keeps[stream][pl.ds(size * LANES, LOG_ROWS), :] = logs
        sends[pl.ds(BASES[stream] + size * LANES, LOG_ROWS), :] = logs


def local_kernel(heads, blocks, part, *refs):
    start, stop = (0, SIZES[0]) if part == 0 else (SIZES[0], blocks)
    if part == 0:
        raw_ref, decay_ref, x_ref, g_ref, b_ref, c_ref = refs[:6]
        outs, (wide, row_t) = refs[6:15], refs[15:]
        raw, step, rate, cumulative = head_terms(raw_ref, decay_ref, wide, heads)
    else:
        x_ref, g_ref, b_ref, c_ref = refs[:4]
        gathered_in, row_in, column_in, skip_in, step_ref, cumulative_ref = refs[4:10]
        outs, (row_t,) = refs[10:16], refs[16:]
        step = step_ref[...]
        cumulative = cumulative_ref[...]
    rows = cumulative.shape[0]
    lane = iota((rows, LANES), 1)
    first = lane < LANES // 2
    causal = iota((rows, rows), 1) >= iota((rows, rows), 0)
    cumulative_t = cumulative.T
    keys = b_ref[...]
    queries = c_ref[...]
    scores_t = jnp.where(causal, nt(keys, queries), 0.0)
    lane_one = iota((1, LANES), 1)
    zero = jnp.zeros((rows, LANES), BF16)
    if part == 0:
        row_t[...] = jnp.zeros_like(row_t)
        gathered = jnp.zeros((rows, rows), F32)
        column_step = jnp.zeros((rows, LANES), F32)
        skip = jnp.zeros((1, LANES), F32)
    else:
        row_t[...] = row_in[...]
        gathered = gathered_in[...]
        column_step = column_in[...]
        skip = skip_in[...]
    for block in range(start, stop):
        place = block - start
        cols = pl.ds(block * LANES, LANES)
        x = x_ref[:, cols]
        g = g_ref[:, cols]
        both_x = jnp.concatenate([jnp.where(first, x, zero), jnp.where(first, zero, x)], axis=0)
        both_g = jnp.concatenate([jnp.where(first, g, zero), jnp.where(first, zero, g)], axis=0)
        products = nt(both_x, g)
        highs, lows = [], []
        for side in range(2):
            head = 2 * block + side
            between = cumulative_t[head : head + 1, :] - cumulative[:, head : head + 1]
            decay = jnp.exp(jnp.minimum(between, 0.0))
            high, low = halves(decay * scores_t)
            highs.append(high)
            lows.append(low)
            scaled = decay * products[side * rows : (side + 1) * rows] * step[:, head : head + 1]
            gathered = gathered + scaled
            scored = scaled * scores_t
            row_t[head : head + 1, :] = jnp.sum(scored, axis=0, keepdims=True)
            column_step = jnp.where(lane == head, jnp.sum(scored, axis=1, keepdims=True), column_step)
        outs[0][:, pl.ds(place * LANES, LANES)] = nn(jnp.concatenate(highs, axis=1), both_g) + nn(
            jnp.concatenate(lows, axis=1), both_g
        )
        met = jnp.sum(x.astype(F32) * g.astype(F32), axis=0, keepdims=True)
        early = jnp.sum(jnp.where(first[:1], met, 0.0), axis=1, keepdims=True)
        late = jnp.sum(jnp.where(first[:1], 0.0, met), axis=1, keepdims=True)
        skip = jnp.where(lane_one == 2 * block, early, skip)
        skip = jnp.where(lane_one == 2 * block + 1, late, skip)
    if part == 0:
        values = (gathered, row_t[...], column_step, skip, step, cumulative, 1.0 / (1.0 + jnp.exp(-raw)), rate)
    else:
        gathered = jnp.where(causal, gathered, 0.0)
        values = (
            nn(jnp.concatenate(halves(gathered), axis=1), jnp.concatenate([queries, queries], axis=0)),
            nn(jnp.concatenate(halves(gathered.T), axis=1), jnp.concatenate([keys, keys], axis=0)),
            row_t[...].T - column_step,
            column_step / step,
            skip,
        )
    for out, value in zip(outs[1:], values):
        out[...] = value


def gradient_kernel(heads, blocks, stream, core_ref, skip_weight_ref, x_ref, g_ref, b_ref, c_ref, *rest):
    fixed, rest = rest[:9], rest[9:]
    (adjoint_ref, through_ref, column_ref, step_ref, cumulative_ref, slope_ref, rate_ref, skip_ref, pair_ref) = fixed
    before_ref, other_ref, rest = rest[0], rest[1], rest[2:]
    given = 2 if stream == 0 else 6
    taken, rest = rest[:given], rest[given:]
    final = stream == STREAMS - 1
    forward = core_ref[0] == 1
    step = step_ref[...]
    cumulative = cumulative_ref[...]
    rows = cumulative.shape[0]
    wide = rest[-1]
    wide[0:1, :] = jnp.zeros((1, LANES), F32)
    wide[0:1, :heads] = skip_weight_ref[...]
    skip_weight = wide[0:1, :]
    closing = cumulative[-1:, :]
    tail = jnp.exp(closing - cumulative)
    lift = jnp.exp(cumulative)
    first = iota((rows, LANES), 1) < LANES // 2
    lane_one = iota((1, LANES), 1)
    keys = jnp.concatenate([b_ref[...], b_ref[...]], axis=1)
    queries = jnp.concatenate([c_ref[...], c_ref[...]], axis=1)
    side = iota((LANES, LANES), 0) // (LANES // 2)
    place_lane = iota((LANES, LANES), 1)
    from_keys = taken[0][...]
    from_queries = taken[1][...]
    if stream == 0:
        outward_sum = jnp.zeros((rows, LANES), F32)
        inward_sum = jnp.zeros((rows, LANES), F32)
        meeting = jnp.zeros((1, LANES), F32)
    else:
        outward_sum = taken[2][...]
        inward_sum = taken[3][...]
        meeting = taken[4][...]
    grad_x = rest[0]
    base, size, start = BASES[stream], SIZES[stream], STARTS[stream]
    if stream > 0:
        ready = pl.ds(0, start * LANES)
        grad_x[:, ready] = taken[5][:, ready]
    for place in range(size):
        block = start + place
        cols = pl.ds(block * LANES, LANES)
        where = pl.ds(place * LANES, LANES)
        log_row = pair_ref[pl.ds(base + size * LANES + place, 1), :]
        mine = pair_ref[pl.ds(base + place * LANES, LANES), :] + jnp.exp(log_row) * before_ref[where, :]
        theirs = other_ref[where, :]
        entering = jnp.where(forward, mine, theirs)
        message = jnp.where(forward, theirs, mine)
        entering_high, entering_low = halves(entering)
        message_high, message_low = halves(message)
        x = x_ref[:, cols].astype(F32)
        g = g_ref[:, cols].astype(F32)
        message_keys = nn(keys, jnp.concatenate([message_high, message_low], axis=0))
        state_queries = nn(queries, jnp.concatenate([entering_high, entering_low], axis=0))
        tail_b = spread(tail, block, first)
        step_b = spread(step, block, first)
        skip_b = spread(skip_weight, block, first[:1])
        weighted_high, weighted_low = halves(tail_b * step_b * x)
        lifted_high, lifted_low = halves(spread(lift, block, first) * g)
        picker = jnp.where(place_lane == side + 2 * block, 1.0, 0.0).astype(BF16)
        picker = jnp.concatenate([picker, picker], axis=0)
        outward_sum = outward_sum + nn(jnp.concatenate(halves(x * message_keys), axis=1), picker)
        inward_sum = inward_sum + nn(jnp.concatenate(halves(g * state_queries), axis=1), picker)
        from_keys = from_keys + (
            nt(
                jnp.concatenate([weighted_high, weighted_low], axis=1),
                jnp.concatenate([message_high, message_high], axis=1),
            )
            + nt(weighted_high, message_low)
        )
        from_queries = from_queries + (
            nt(
                jnp.concatenate([lifted_high, lifted_low], axis=1),
                jnp.concatenate([entering_high, entering_high], axis=1),
            )
            + nt(lifted_high, entering_low)
        )
        met = jnp.sum(entering * message, axis=0, keepdims=True)
        early = jnp.sum(jnp.where(first[:1], met, 0.0), axis=1, keepdims=True)
        late = jnp.sum(jnp.where(first[:1], 0.0, met), axis=1, keepdims=True)
        meeting = jnp.where(lane_one == 2 * block, early, meeting)
        meeting = jnp.where(lane_one == 2 * block + 1, late, meeting)
        near = pl.ds((block if stream == 0 else block - SIZES[0]) * LANES, LANES)
        grad = step_b * (adjoint_ref[:, near] + tail_b * message_keys) + skip_b * g
        grad_x[:, cols] = grad.astype(grad_x.dtype)
    rest[1][...] = from_keys
    rest[2][...] = from_queries
    if not final:
        rest[3][...] = outward_sum
        rest[4][...] = inward_sum
        rest[5][...] = meeting
        return
    grad_raw, sums = rest[3], rest[4]
    rate = rate_ref[...]
    inward = lift * inward_sum
    lead = tail * outward_sum
    outward = lead * step
    through = through_ref[...] + inward - outward
    last = jnp.sum(outward, axis=0, keepdims=True) + jnp.exp(closing) * meeting
    through = through + jnp.where(iota((rows, LANES), 0) == rows - 1, last, 0.0)
    upper = (iota((rows, rows), 1) >= iota((rows, rows), 0)).astype(F32)
    grad_cumulative = jnp.dot(upper, through, precision=HIGHEST, preferred_element_type=F32)
    grad_step = grad_cumulative * rate + column_ref[...] + lead
    grad_raw[...] = (grad_step * slope_ref[...]).T[:heads, :]
    rate_sum = jnp.sum(grad_cumulative * step, axis=0, keepdims=True) * rate
    wide[0:1, :] = jnp.where(lane_one < heads, rate_sum, 0.0)
    wide[0:1, LANES // 2 :] = skip_ref[:, : LANES // 2]
    sums[...] = jnp.broadcast_to(wide[0:1, :], sums.shape)


def combine_kernel(size, has_before, wants_send, *refs):
    refs = list(refs)
    own = refs.pop(0) if wants_send else None
    past = refs.pop(0) if has_before else None
    arrived = refs.pop(0)
    new_past = refs.pop(0) if has_before else None
    send = refs.pop(0) if wants_send else None
    tail = pl.ds(size * LANES, LOG_ROWS)
    past_log = past[tail, :] if has_before else None
    new_log = arrived[tail, :] + past_log if has_before else arrived[tail, :]
    if has_before:
        new_past[tail, :] = new_log
        past_decay = jnp.exp(past_log)
    if wants_send:
        own_log = own[tail, :]
        own_decay = jnp.exp(own_log)
        send[tail, :] = own_log + new_log
    for place in range(size):
        where = pl.ds(place * LANES, LANES)
        state = arrived[where, :]
        if has_before:
            state = past[where, :] + past_decay[place : place + 1, :] * state
            new_past[where, :] = state
        if wants_send:
            send[where, :] = own[where, :] + own_decay[place : place + 1, :] * state


def chip_moves(moves, chips):
    ahead = [(2 * a + 1, 2 * b + 1) for a, b in moves]
    back = [(2 * (chips - 1 - a), 2 * (chips - 1 - b)) for a, b in moves]
    return ahead + back


ROUNDS = (
    [(z, z + 1) for z in range(0, 16, 2)],
    [(1, 3), (5, 7), (9, 11)],
    [(3, 7), (1, 2)],
    [(7, 11), (3, 5)],
    [(11, 13), (7, 9), (5, 6), (3, 4)],
    [(7, 8), (9, 10), (11, 12), (13, 14)],
)
LAST_CHIP = [(13, 15)]


def combine(size, own, past, arrived):
    shape = jax.ShapeDtypeStruct(arrived.shape, F32)
    operands = [a for a in (own, past, arrived) if a is not None]
    whole = pl.BlockSpec(memory_space=pltpu.VMEM)
    outs = (past is not None) + (own is not None)
    results = list(
        pl.pallas_call(
            functools.partial(combine_kernel, size, past is not None, own is not None),
            out_shape=[shape] * outs,
            in_specs=[whole] * len(operands),
            out_specs=[whole] * outs,
            compiler_params=pltpu.CompilerParams(vmem_limit_bytes=8 * 1024 * 1024),
            cost_estimate=pl.CostEstimate(flops=1_000_000, bytes_accessed=1_000_000, transcendentals=0),
            name="combine",
        )(*operands)
    )
    new_past = results.pop(0) if past is not None else arrived
    return new_past, (results.pop(0) if own is not None else None)


def first_kernel(*refs):
    keeps, pair, owns = refs[:STREAMS], refs[STREAMS], refs[STREAMS + 1 :]
    for keep, own, base, size in zip(keeps, owns, BASES, SIZES):
        tail = pl.ds(size * LANES, LOG_ROWS)
        log = keep[tail, :]
        decay = jnp.exp(log)
        own[tail, :] = log + pair[pl.ds(base + size * LANES, LOG_ROWS), :]
        for place in range(size):
            where = pl.ds(place * LANES, LANES)
            own[where, :] = keep[where, :] + decay[place : place + 1, :] * pair[pl.ds(base + place * LANES, LANES), :]


def scan_chips(keeps, pair, swap, within, gradients):
    chips = 16
    whole = pl.BlockSpec(memory_space=pltpu.VMEM)
    own = pl.pallas_call(
        first_kernel,
        out_shape=[jax.ShapeDtypeStruct(keep.shape, F32) for keep in keeps],
        in_specs=[whole] * (STREAMS + 1),
        out_specs=[whole] * STREAMS,
        compiler_params=pltpu.CompilerParams(vmem_limit_bytes=8 * 1024 * 1024),
        cost_estimate=pl.CostEstimate(flops=1_000_000, bytes_accessed=4_000_000, transcendentals=0),
        name="pair_up",
    )(*keeps, pair)
    send, past = list(own), [None] * STREAMS
    final = len(ROUNDS) - 1
    carried = None
    for turn, moves in enumerate(ROUNDS):
        arrived = []
        for stream in range(STREAMS):
            got = [lax.ppermute(send[stream], "ctx", chip_moves(moves, chips))]
            if turn == final:
                got.append(lax.ppermute(send[stream], "ctx", chip_moves(LAST_CHIP, chips)))
            arrived.append(got)
        if turn == 0:
            local = within(own[-1])
            arrived[-1], local = lax.optimization_barrier((arrived[-1], local))
        if turn > 0:
            arrived[0], _ = lax.optimization_barrier((arrived[0], previous))
        previous = arrived[-1]
        for stream in range(STREAMS):
            if turn == final and stream == STREAMS - 1 and stream > 0:
                arrived[stream], carried = lax.optimization_barrier((arrived[stream], carried))
            for block in arrived[stream]:
                target = own[stream] if turn < final else None
                past[stream], new_send = combine(SIZES[stream], target, past[stream], block)
                send[stream] = new_send if new_send is not None else send[stream]
            if turn == final:
                other = lax.ppermute(past[stream], "ctx", swap)
                carried = gradients(stream, local, past[stream], other, carried)
    return carried


def per_device(inputs, in_keys, output_queries, step_raw, decay_log, skip_weight, grad_out):
    rows = inputs.shape[1]
    width = inputs.shape[2]
    heads = decay_log.shape[0]
    blocks = width // LANES
    count = lax.axis_size("ctx")
    swap = [(i, i ^ 1) for i in range(count)]
    core = lax.rem(lax.axis_index("ctx"), 2).astype(jnp.int32).reshape(1)
    x, g, keys, queries = inputs[0], grad_out[0], in_keys[0], output_queries[0]
    raw_t = jnp.swapaxes(step_raw[0], 0, 1)
    decay_row = decay_log.reshape(1, heads)
    skip_row = skip_weight.reshape(1, heads)
    whole = pl.BlockSpec(memory_space=pltpu.VMEM)
    scalar = pl.BlockSpec(memory_space=pltpu.SMEM)
    params = pltpu.CompilerParams(vmem_limit_bytes=VMEM_LIMIT)
    tile = jax.ShapeDtypeStruct((rows, LANES), F32)
    line = jax.ShapeDtypeStruct((1, LANES), F32)
    packed = [jax.ShapeDtypeStruct((count_rows, LANES), F32) for count_rows in (*ROWS, sum(ROWS))]
    wide = pltpu.VMEM((rows, LANES), F32)

    operands = (raw_t, decay_row, x, g, keys, queries)
    far = pl.BlockSpec(memory_space=pltpu.HBM)
    made = pl.pallas_call(
        functools.partial(summary_kernel, heads, blocks),
        out_shape=packed,
        in_specs=[scalar] + [far] * 6,
        out_specs=[whole] * (STREAMS + 1),
        scratch_shapes=[pltpu.VMEM(a.shape, a.dtype) for a in operands]
        + [wide, pltpu.SemaphoreType.DMA((6,))],
        compiler_params=params,
        cost_estimate=pl.CostEstimate(flops=400_000_000, bytes_accessed=4_000_000, transcendentals=0),
        name="summaries",
    )(core, *operands)
    keeps, sends = made[:STREAMS], made[STREAMS]

    parts = [jax.ShapeDtypeStruct((rows, n * LANES), F32) for n in (SIZES[0], blocks - SIZES[0])]
    row_scratch = pltpu.VMEM((LANES, rows), F32)

    def local_part(part, held, out_shape, scratch):
        return pl.pallas_call(
            functools.partial(local_kernel, heads, blocks, part),
            out_shape=out_shape,
            in_specs=[whole] * len(held),
            out_specs=[whole] * len(out_shape),
            scratch_shapes=scratch,
            compiler_params=params,
            cost_estimate=pl.CostEstimate(flops=1_000_000_000, bytes_accessed=3_000_000, transcendentals=0),
            name="within_slab",
        )(*held)

    held, keeps = lax.optimization_barrier((operands, keeps))
    pair = lax.ppermute(sends, "ctx", swap)
    early = local_part(0, held, [parts[0]] + [tile] * 3 + [line] + [tile] * 3 + [line], [wide, row_scratch])
    pair, early = lax.optimization_barrier((pair, early))

    def within_slab(after):
        again, _ = lax.optimization_barrier(((*operands[2:], *early[1:7]), after))
        late = local_part(1, again, [parts[1]] + [tile] * 4 + [line], [row_scratch])
        return [early[0], late[0], *late[1:5], *early[5:9], late[5]]

    full = jax.ShapeDtypeStruct((rows, width), BF16)

    def gradients(stream, local, before, other, carried):
        final = stream == STREAMS - 1
        shapes = [full, tile, tile]
        if final:
            shapes += [jax.ShapeDtypeStruct((heads, rows), F32), jax.ShapeDtypeStruct((count, LANES), F32)]
        else:
            shapes += [tile, tile, line]
        adjoint = local[0] if stream == 0 else local[1]
        keys_part, queries_part, *terms = local[2:]
        carried = [keys_part, queries_part] if carried is None else [*carried[1:], carried[0]]
        given = [core, skip_row, x, g, keys, queries, adjoint, *terms, pair, before, other, *carried]
        return pl.pallas_call(
            functools.partial(gradient_kernel, heads, blocks, stream),
            out_shape=shapes,
            in_specs=[scalar] + [whole] * (len(given) - 1),
            out_specs=[whole] * len(shapes),
            scratch_shapes=[pltpu.VMEM((8, LANES), F32)],
            compiler_params=params,
            cost_estimate=pl.CostEstimate(flops=800_000_000, bytes_accessed=8_000_000, transcendentals=0),
            name="gradients",
        )(*given)

    done = scan_chips(keeps, pair, swap, within_slab, gradients)
    grad_x, grad_keys, grad_queries, grad_raw_t, shared = done
    shared = lax.all_to_all(shared, "ctx", 0, 0, tiled=True)
    line_sum = jnp.sum(shared, axis=0)
    shared = jnp.broadcast_to(line_sum[None], (lax.axis_size("dp"), LANES))
    line_sum = jnp.sum(lax.all_to_all(shared, "dp", 0, 0, tiled=True), axis=0)
    return (
        grad_x[None],
        grad_keys[None],
        grad_queries[None],
        jnp.swapaxes(grad_raw_t, 0, 1)[None],
        line_sum[:heads],
        line_sum[LANES // 2 : LANES // 2 + heads],
    )


def solution(mesh):
    placed = P("dp", "ctx", None)
    return jax.shard_map(
        per_device,
        mesh=mesh,
        in_specs=(placed, placed, placed, placed, P(), P(), placed),
        out_specs=(placed, placed, placed, placed, P(), P()),
        check_vma=False,
    )
```
